256 devices in a mesh: grp: 16 (over z, y_hi), ep: 16 (over y_lo, x, core).
Axes of the slice: x: 4, y: 4 (y_hi: 2, y_lo: 2; y = y_hi * 2 + y_lo), z: 8, core: 2. Of those that a mesh axis runs over, the one named last changes fastest.
Arguments:
- tokens: bfloat16 [49152, 4096], P(('grp', 'ep')), may hold values from -6 to 6
- expert_ids: int32 [49152, 8], P(('grp', 'ep')), may hold values from 0 to 127, all different within a row; in each aligned block of 192 rows (0 to 191, 192 to 383, ...) at most 24 rows name the same one
- gate_probs: float32 [49152, 8], P(('grp', 'ep')), may hold values from 0.02 to 0.25
- placement: int32 [16, 4], P('grp'), may hold values from 0 to 1
- gate_weight: bfloat16 [16, 4096, 3072], P('grp', None, 'ep'), may hold values from -0.09375 to 0.09375
- up_weight: bfloat16 [16, 4096, 3072], P('grp', None, 'ep'), may hold values from -0.09375 to 0.09375
- down_weight: bfloat16 [16, 3072, 4096], P('grp', 'ep'), may hold values from -0.21875 to 0.21875
- out_grad: bfloat16 [49152, 4096], P(('grp', 'ep')), may hold values from -6 to 6
- moment_first: float32 [2, 3072, 4096], P(None, 'ep', 'grp'), may hold values from -2 to 2
- moment_second: float32 [2, 3072, 4096], P(None, 'ep', 'grp'), may hold values from 0.01 to 1
Outputs:
- token_grad: bfloat16 [49152, 4096], P(('grp', 'ep'))
- step_dir: bfloat16 [16, 3072, 4096], P('grp', 'ep')
- new_first: float32 [2, 3072, 4096], P(None, 'ep', 'grp')
- new_second: float32 [2, 3072, 4096], P(None, 'ep', 'grp')
The draws below stay inside these ranges and needn't reach their ends.
Inputs may be any that keep to these rules, and one draw needn't show every extreme that they name: `expert_ids`: each row names 8 different experts. In the rows of one device no expert is named more than 24 times, a bound that some block reaches. Group g holds expert placement[g, s] * 4 + s in its slot s.
All inputs are finite; a program needn't handle non-finite values.
Results may differ from the reference program's by a relative error of at most 0.015.
Values may be sent and summed in bfloat16 or wider, within the bound.
A program may use at most 128 MiB of HBM per device.

```python
import math
import jax
import jax.numpy as jnp
import numpy as np
from jax import lax

D = 4096
HID = 768
EXPERTS = 128
TOP = 8
QUARTERS = 4
CANDS = 2
TOK_DEV = 192
SLOTS = 4
H_DEV = 192
CAP = 24
TOKENS = 49152
N_GRP = 16
N_EP = 16


def with_ends(result, own_key, least, top_value):
    dims = result.shape
    place = [jax.random.randint(jax.random.fold_in(own_key, axis), (), 0, dims[axis]) for axis in range(len(dims))]
    result = result.at[tuple(place)].set(least)
    longest = dims.index(max(dims))
    place[longest] = (place[longest] + 1) % dims[longest]
    return result.at[tuple(place)].set(top_value)


def levels(key, dims, shards, low, largest):
    def one(axis_at, blocks):
        draws = jax.random.uniform(jax.random.fold_in(jax.random.fold_in(key, 6), axis_at), (blocks,), jnp.float32, low / len(shards), largest / len(shards))
        return jnp.repeat(jnp.exp(draws), dims[axis_at] // blocks).reshape((-1,) + (1,) * (len(dims) - axis_at - 1))

    loudness = one(*shards[0])
    for cut in shards[1:]:
        loudness = loudness * one(*cut)
    return loudness


def shared_out(key, own, number, rows, amount, top, reach, slope):
    order = jax.random.permutation(key, amount)
    packed, usual = portions_of(amount, rows * top, reach, slope, True), portions_of(amount, rows * top, reach, slope, False)
    places = jnp.arange(amount)

    def named(tallies, turn):
        used = int((tallies > 0).sum())
        fixed = max(1, used // 4)
        moved = fixed + (places - fixed + turn * (used - fixed)) % max(1, amount - fixed)
        return jnp.zeros((amount,), jnp.int32).at[order[jnp.where(places < fixed, places, moved)]].set(jnp.asarray(tallies, jnp.int32))

    tallies = jnp.where(number % 4 == 0, named(packed, number // 4), named(usual, number - number // 4 - 1))
    mixed = jax.random.permutation(jax.random.fold_in(own, 3), amount)
    source_of, receiver = mixed[0:amount // 2 * 2:2], mixed[1:amount // 2 * 2:2]
    slack = jnp.minimum(tallies[source_of] - 1, reach - tallies[receiver]) // 2
    slack = jnp.where((source_of == order[0]) | (receiver == order[0]) | (tallies[receiver] == 0), 0, jnp.maximum(slack, 0))
    moved = jax.random.randint(jax.random.fold_in(own, 4), (amount // 2,), 0, 1 << 20) % (slack + 1)
    tallies = tallies.at[source_of].add(-moved).at[receiver].add(moved)
    members = jnp.searchsorted(jnp.cumsum(tallies), jnp.arange(rows * top), side="right").astype(jnp.int32)
    table = members.reshape(top, rows).T
    table = table[jax.random.permutation(jax.random.fold_in(own, 1), rows)]
    turn = jax.random.randint(jax.random.fold_in(own, 2), (rows, 1), 0, top)
    return jnp.take_along_axis(table, (jnp.arange(top)[None, :] + turn) % top, axis=1)


def portions_of(count, total, limit, skew, full):
    weights = [(1 << 20) // math.isqrt(grade ** skew) + 1 for grade in range(1, count + 1)]
    largest = limit if full else min(limit, max(-(-total // count), total * weights[0] // sum(weights)))
    least = 1 if total - largest >= count - 1 else 0
    counts, surplus = [largest] + [least] * (count - 1), total - largest - least * (count - 1)
    while surplus > 0:
        movable = [i for i in range(1, count) if counts[i] < largest] or [i for i in range(1, count) if counts[i] < limit]
        mass, budget = sum([weights[i] for i in movable]), surplus
        for i in movable:
            extra = min(limit - counts[i], max(1, budget * weights[i] // mass), surplus)
            counts[i] = counts[i] + extra
            surplus = surplus - extra
    return np.array(counts)


def scatter_about(key, dims, deviation, bound, split=(), held_as=jnp.bfloat16):
    entries = deviation * jax.random.normal(key, dims, jnp.float32)
    if split:
        entries = entries * levels(key, dims, split, -0.22, 0.18)
    return jnp.clip(entries, -bound, bound).astype(held_as)


def setup_inputs(seed: int = 0) -> dict:
    arg_keys = jax.random.split(jax.random.key(seed), 11)
    tokens = scatter_about(arg_keys[0], (TOKENS, D), 1.0, 6.0, ((0, 256),))
    expert_ids_keys = jax.random.split(jax.random.fold_in(arg_keys[1], 1), TOKENS // TOK_DEV)
    expert_ids_turns = jax.random.permutation(jax.random.fold_in(arg_keys[1], 3), TOKENS // TOK_DEV)
    expert_ids = jax.vmap(lambda own, number: shared_out(jax.random.fold_in(arg_keys[1], 2), own, number, TOK_DEV, EXPERTS, TOP, CAP, 2))(expert_ids_keys, expert_ids_turns).reshape((TOKENS, TOP))
    gate_probs = jnp.clip(0.02 + 0.23 * jax.random.uniform(arg_keys[2], (TOKENS, TOP), jnp.float32) ** levels(arg_keys[2], (TOKENS, TOP), ((0, 256),), -0.2, 0.2), 0.02, 0.25)
    placement = with_ends(jax.random.randint(arg_keys[3], (N_GRP, SLOTS), 0, CANDS), jax.random.fold_in(arg_keys[3], 1), 0, CANDS - 1).astype(jnp.int32)
    gate_weight = scatter_about(arg_keys[4], (N_GRP, D, N_EP * H_DEV), D ** -0.5, 0.09375, ((0, 16), (2, 16)))
    up_weight = scatter_about(arg_keys[5], (N_GRP, D, N_EP * H_DEV), D ** -0.5, 0.09375, ((0, 16), (2, 16)))
    down_weight = scatter_about(arg_keys[6], (N_GRP, N_EP * H_DEV, D), HID ** -0.5, 0.21875, ((0, 16), (1, 16)))
    out_grad = scatter_about(arg_keys[7], (TOKENS, D), 1.0, 6.0, ((0, 256),))
    moment_first = scatter_about(arg_keys[8], (CANDS, N_EP * H_DEV, D), 0.3, 2.0, ((1, 16), (2, 16)), jnp.float32)
    moment_second = jnp.clip(jnp.exp(math.log(1.0) - 4.6051702 * jax.random.uniform(arg_keys[9], (CANDS, N_EP * H_DEV, D), jnp.float32) ** levels(arg_keys[9], (CANDS, N_EP * H_DEV, D), ((1, 16), (2, 16)), -0.2, 0.2)), 0.01, 1.0)
    return dict(tokens=tokens, expert_ids=expert_ids, gate_probs=gate_probs, placement=placement, gate_weight=gate_weight, up_weight=up_weight, down_weight=down_weight, out_grad=out_grad, moment_first=moment_first, moment_second=moment_second)


beta_one = 0.9
beta_two = 0.999
adam_eps = 1e-08
first_fix = 1.0 - math.exp(1000.0 * math.log(0.9))
second_fix = 1.0 - math.exp(1000.0 * math.log(0.999))

def adam_step(gradient, first_moment, second):
    new_first = beta_one * first_moment + (1.0 - beta_one) * gradient
    new_second = beta_two * second + (1.0 - beta_two) * gradient * gradient
    direction = new_first / first_fix / (jnp.sqrt(new_second / second_fix) + adam_eps)
    return (new_first, new_second, direction)

def one_group(inputs):
    tok_rows, id_rows, prob_rows, grad_rows, place_row, gate_group, up_group, down_group = inputs
    count_rows = tok_rows.shape[0]
    token_acc = jnp.zeros((count_rows, D), jnp.float32)
    grad_list = []
    for slot_index in range(SLOTS):
        expert = place_row[slot_index] * SLOTS + slot_index
        matches = id_rows == expert
        coeffs = lax.optimization_barrier(jnp.sum(jnp.where(matches, prob_rows, jnp.float32(0.0)), axis=1))
        hit_rows = jnp.any(matches, axis=1)
        chosen = jnp.nonzero(hit_rows, size=N_EP * CAP, fill_value=0)[0].astype(jnp.int32)
        valid = jnp.arange(N_EP * CAP, dtype=jnp.int32) < jnp.sum(hit_rows.astype(jnp.int32))
        sel_coeffs = jnp.where(valid, coeffs[chosen], jnp.float32(0.0))
        sel_tokens = tok_rows[chosen]
        sel_grads = grad_rows[chosen]
        w_gate = gate_group[:, slot_index * HID:(slot_index + 1) * HID]
        w_up = up_group[:, slot_index * HID:(slot_index + 1) * HID]
        w_down = down_group[slot_index * HID:(slot_index + 1) * HID, :]
        pre_gate = jnp.dot(sel_tokens, w_gate, preferred_element_type=jnp.float32)
        pre_up = jnp.dot(sel_tokens, w_up, preferred_element_type=jnp.float32)
        sigmoid_gate = jax.nn.sigmoid(pre_gate)
        activated = pre_gate * sigmoid_gate
        hidden = (activated * pre_up).astype(jnp.bfloat16)
        scaled = (sel_coeffs[:, None] * sel_grads.astype(jnp.float32)).astype(jnp.bfloat16)
        d_hidden = jnp.dot(scaled, w_down.T, preferred_element_type=jnp.float32)
        grad_list.append(jnp.dot(hidden.T, scaled, preferred_element_type=jnp.float32))
        d_gate = (d_hidden * pre_up * sigmoid_gate * (1.0 + pre_gate * (1.0 - sigmoid_gate))).astype(jnp.bfloat16)
        d_up = (d_hidden * activated).astype(jnp.bfloat16)
        quarter_sum = jnp.zeros((N_EP * CAP, D), jnp.float32)
        for quarter in range(QUARTERS):
            low = quarter * H_DEV
            high = low + H_DEV
            partial_value = jnp.dot(d_gate[:, low:high], w_gate[:, low:high].T, preferred_element_type=jnp.float32)
            partial_value = partial_value + jnp.dot(d_up[:, low:high], w_up[:, low:high].T, preferred_element_type=jnp.float32)
            rounded = lax.optimization_barrier(partial_value.astype(jnp.bfloat16))
            quarter_sum = quarter_sum + rounded.astype(jnp.float32)
        token_acc = token_acc.at[chosen].add(quarter_sum)
    return (token_acc.astype(jnp.bfloat16), jnp.stack(grad_list))

def reference(tokens, expert_ids, gate_probs, placement, gate_weight, up_weight, down_weight, out_grad, moment_first, moment_second):
    group_rows = N_EP * TOK_DEV
    per_group = (tokens.reshape(N_GRP, group_rows, D), expert_ids.reshape(N_GRP, group_rows, TOP), gate_probs.reshape(N_GRP, group_rows, TOP), out_grad.reshape(N_GRP, group_rows, D), placement, gate_weight, up_weight, down_weight)
    token_grad, slot_grads = lax.map(one_group, per_group)
    chosen_cands = (placement[:, :, None] == jnp.arange(CANDS, dtype=jnp.int32)[None, None, :]).astype(jnp.float32)
    summed = jnp.einsum('gsr,gshd->rshd', chosen_cands, slot_grads, precision=lax.Precision.HIGHEST)
    summed = summed.reshape(CANDS, SLOTS * HID, D)
    new_first, new_second, direction = adam_step(summed, moment_first, moment_second)
    copy_dirs = jnp.einsum('gsr,rshd->gshd', chosen_cands, direction.reshape(CANDS, SLOTS, HID, D), precision=lax.Precision.HIGHEST)
    step_dir = copy_dirs.reshape(N_GRP, SLOTS * HID, D).astype(jnp.bfloat16)
    return (token_grad.reshape(N_GRP * group_rows, D), step_dir, new_first, new_second)
```

```python
import math

import jax
import jax.numpy as jnp
from jax import lax
from jax.experimental import pallas as pl
from jax.experimental.pallas import tpu as pltpu
from jax.sharding import PartitionSpec as P

MESH = pl.DeviceIdType.MESH
F32 = jnp.float32
BF16 = jnp.bfloat16

D = 4096
HALF = 2048
TOK = 192
HU = 192
CAP = 24
PAIR = 2 * CAP
SLOTS = 4
CHIPS = 8
NX = 4
NZ = 8
SHARE = 256
ROWS = CHIPS * PAIR
CH = 512

beta_one = 0.9
beta_two = 0.999
adam_eps = 1e-08
first_fix = 1.0 - math.exp(1000.0 * math.log(0.9))
second_fix = 1.0 - math.exp(1000.0 * math.log(0.999))

OFFS = [(dy, dx) for dx in (2, 1, 3, 0) for dy in (1, 0) if (dy, dx) != (0, 0)]
NO = len(OFFS)
NT = (((1,), (1,)), ((), ()))


def body(
    tok, ids, prb, plc, wg, wu, wd, og, m1, m2,
    tg_out, sd_out, nf_out, ns_out,
    tokH, grdH, idsH, prbH, hm, cm, sel_t, snd_t, snd_g, xt, xg,
    wgv, wuv, wdv, m1v, m2v, hid_t, dgv, duv,
    p_snd, p_rcv, p_own, r_snd, r_rcv, tgv,
    mine, theirs, wy_snd, wy_rcv, w_own,
    rm_snd, rm_rcv, rp_snd, rp_rcv, dall, ds, dy,
    lsem, s_in, r_in, s_t, r_t, f_t, g_t, s_g, r_g, f_g, g_g,
    s_p, r_p, s_r, r_r, s_tg, r_tg,
    s_c, r_c, s_y, r_y, s_m, r_m, s_q, r_q, s_am, r_am, s_ap, r_ap, s_d, r_d, l_d,
):
    g = lax.axis_index("grp")
    e = lax.axis_index("ep")
    z, yh = g // 2, lax.rem(g, 2)
    q, k = e // 2, lax.rem(e, 2)
    yl, x = q // NX, lax.rem(q, NX)
    slot = q // 2
    sib = {"grp": g, "ep": q * 2 + 1 - k}
    ypart = {"grp": z * 2 + 1 - yh, "ep": e}
    zup = {"grp": lax.rem(z + 1, NZ) * 2 + yh, "ep": e}
    zdn = {"grp": lax.rem(z + NZ - 1, NZ) * 2 + yh, "ep": e}

    def chip(off, sign):
        return lax.rem(yl + off[0], 2) * NX + lax.rem(x + sign * off[1] + NX, NX)

    def remote(src, dst, ssem, rsem, to):
        return pltpu.make_async_remote_copy(
            src_ref=src, dst_ref=dst, send_sem=ssem, recv_sem=rsem, device_id=to,
            device_id_type=MESH,
        )

    def cols(i):
        return pl.ds(pl.multiple_of(i * SHARE, SHARE), SHARE)

    mine_cols = pl.ds(pl.multiple_of(k * HALF, HALF), HALF)
    other_cols = pl.ds(pl.multiple_of((1 - k) * HALF, HALF), HALF)

    local = [
        pltpu.make_async_copy(ids, idsH.at[k], lsem.at[0]),
        pltpu.make_async_copy(prb, prbH.at[k], lsem.at[1]),
        pltpu.make_async_copy(tok.at[:, mine_cols], tokH.at[k], lsem.at[2]),
        pltpu.make_async_copy(og.at[:, mine_cols], grdH.at[k], lsem.at[3]),
    ]
    later = [
        pltpu.make_async_copy(wg.at[0], wgv, lsem.at[4]),
        pltpu.make_async_copy(wu.at[0], wuv, lsem.at[5]),
        pltpu.make_async_copy(wd.at[0], wdv, lsem.at[6]),
        pltpu.make_async_copy(m1, m1v, lsem.at[7]),
        pltpu.make_async_copy(m2, m2v, lsem.at[8]),
    ]
    for cp in local + later:
        cp.start()
    mine[...] = jnp.zeros((8, 128), jnp.int32) + plc[0, slot]

    barrier = pltpu.get_barrier_semaphore()
    greet = [sib, ypart, zup, zdn]
    greet += [{"grp": g, "ep": chip(o, 1) * 2 + k} for o in OFFS]
    for to in greet:
        pl.semaphore_signal(barrier, inc=1, device_id=to, device_id_type=MESH)
    pl.semaphore_wait(barrier, len(greet))

    swap = [
        remote(ids, idsH.at[k], s_in.at[0], r_in.at[0], sib),
        remote(prb, prbH.at[k], s_in.at[1], r_in.at[1], sib),
        remote(tok.at[:, other_cols], tokH.at[k], s_in.at[2], r_in.at[2], sib),
        remote(og.at[:, other_cols], grdH.at[k], s_in.at[3], r_in.at[3], sib),
    ]
    for cp in swap:
        cp.start()
    cand_copy = remote(mine, theirs, s_c.at[0], r_c.at[0], ypart)
    cand_copy.start()

    for i in (0, 1):
        local[i].wait()
        swap[i].wait()
    lane = lax.broadcasted_iota(jnp.int32, (TOK, 128), 1)
    for kk in (0, 1):
        id_rows, prob_rows = idsH[kk], prbH[kk]
        hits = jnp.zeros((TOK, 128), F32)
        coefs = jnp.zeros((TOK, 128), F32)
        for s in range(SLOTS):
            match = id_rows == plc[0, s] * SLOTS + s
            hit = jnp.max(jnp.where(match, 1.0, 0.0), axis=1, keepdims=True)
            coef = jnp.sum(jnp.where(match, prob_rows, 0.0), axis=1, keepdims=True)
            hits = jnp.where(lane == s, hit, hits)
            coefs = jnp.where(lane == s, coef, coefs)
        hm[kk * TOK : (kk + 1) * TOK, :] = hits
        cm[kk * TOK : (kk + 1) * TOK, :] = coefs
    hit_r = jnp.transpose(hm[...])[0:8]
    coef_r = jnp.transpose(cm[...])[0:8]
    row = lax.broadcasted_iota(jnp.int32, (2 * TOK, 2 * TOK), 0)
    col = lax.broadcasted_iota(jnp.int32, (2 * TOK, 2 * TOK), 1)
    before = (row < col) & ((row >= TOK) == (col >= TOK))
    before = jnp.where(before, 1.0, 0.0).astype(BF16)
    rank_r = jnp.dot(hit_r.astype(BF16), before, preferred_element_type=F32)
    r48 = lax.broadcasted_iota(jnp.int32, (PAIR, 2 * TOK), 0)
    t48 = lax.broadcasted_iota(jnp.int32, (PAIR, 2 * TOK), 1)
    same = (r48 >= CAP) == (t48 >= TOK)
    place = jnp.where(r48 >= CAP, r48 - CAP, r48).astype(F32)
    picks, scales = [], []
    for s in range(SLOTS):
        ok = same & (hit_r[s : s + 1] > 0.5) & (rank_r[s : s + 1] == place)
        pick = jnp.where(ok, 1.0, 0.0)
        picks.append(pick)
        scales.append(jnp.sum(pick * coef_r[s : s + 1], axis=1, keepdims=True))
    pick_all = jnp.concatenate(picks, axis=0)
    scale_all = jnp.concatenate(scales, axis=0)
    sel_t[...] = jnp.transpose(pick_all).astype(BF16)
    pick_all = pick_all.astype(BF16)

    def select(src, out, scale):
        for c in range(0, HALF, CH):
            rows = src[:, :, c : c + CH].reshape(2 * TOK, CH)
            got = jnp.dot(pick_all, rows, preferred_element_type=F32)
            if scale is not None:
                got = got * scale
            out[:, :, c : c + CH] = got.astype(BF16).reshape(SLOTS, PAIR, CH)

    def dispatch(out, dst, ssem, rsem, fs, fr):
        sends = []
        for i, o in enumerate(OFFS):
            there = chip(o, 1)
            sends.append(remote(out.at[there // 2], dst.at[k, q], ssem.at[i], rsem.at[i],
                                {"grp": g, "ep": there * 2 + k}))
        own = pltpu.make_async_copy(out.at[slot], dst.at[k, q], ssem.at[NO])
        across = remote(out.at[slot], dst.at[k, q], fs.at[NO], fr.at[NO], sib)
        for cp in sends:
            cp.start()
        own.start()
        across.start()
        return sends, own, across

    def arrive(sends, own, across, dst, fs, fr):
        forwards = []
        for i in reversed(range(NO)):
            here = chip(OFFS[i], -1)
            sends[i].wait_recv()
            cp = remote(dst.at[k, here], dst.at[k, here], fs.at[i], fr.at[i], sib)
            cp.start()
            forwards.append(cp)
        for cp in forwards:
            cp.wait()
        across.wait()
        own.wait()
        for cp in sends:
            cp.wait_send()

    local[2].wait()
    swap[2].wait()
    select(tokH, snd_t, None)
    tok_copies = dispatch(snd_t, xt, s_t, r_t, f_t, g_t)
    local[3].wait()
    swap[3].wait()
    select(grdH, snd_g, scale_all)
    grd_copies = dispatch(snd_g, xg, s_g, r_g, f_g, g_g)
    for cp in later:
        cp.wait()
    cand_copy.wait()

    arrive(*tok_copies, xt, f_t, g_t)
    pre_gate = jnp.zeros((ROWS, HU), F32)
    pre_up = jnp.zeros((ROWS, HU), F32)
    for c in range(0, D, CH):
        rows = xt[c // HALF, :, :, c % HALF : c % HALF + CH].reshape(ROWS, CH)
        pre_gate += jnp.dot(rows, wgv[c : c + CH, :], preferred_element_type=F32)
        pre_up += jnp.dot(rows, wuv[c : c + CH, :], preferred_element_type=F32)
    sig = jax.nn.sigmoid(pre_gate)
    act = pre_gate * sig
    hid_t[...] = jnp.transpose(act * pre_up).astype(BF16)

    arrive(*grd_copies, xg, f_g, g_g)

    def grad_share(zd, yd):
        share = zd * 2 + yd
        at = pl.ds(pl.multiple_of(lax.rem(share, 8) * SHARE, SHARE), SHARE)
        rows = xg[share // 8, :, :, at].reshape(ROWS, SHARE)
        return jnp.dot(hid_t[...], rows, preferred_element_type=F32).astype(BF16)

    order = [4, 3, 5, 2, 6, 1, 7, 0]
    y_copies = []
    for n, up in enumerate(order):
        wy_snd[n] = grad_share(lax.rem(z + up, NZ), 1 - yh)
        cp = remote(wy_snd.at[n], wy_rcv.at[n], s_y.at[n], r_y.at[n], ypart)
        cp.start()
        y_copies.append(cp)

    d_hidden = jnp.zeros((ROWS, HU), F32)
    for c in range(0, D, CH):
        rows = xg[c // HALF, :, :, c % HALF : c % HALF + CH].reshape(ROWS, CH)
        d_hidden += lax.dot_general(rows, wdv[:, c : c + CH], NT, preferred_element_type=F32)
    dgv[...] = (d_hidden * pre_up * sig * (1.0 + pre_gate * (1.0 - sig))).astype(BF16)
    duv[...] = (d_hidden * act).astype(BF16)

    def partial(start):
        at = pl.ds(pl.multiple_of(start, CH), CH)
        got = lax.dot_general(dgv[...], wgv[at, :], NT, preferred_element_type=F32)
        return got + lax.dot_general(duv[...], wuv[at, :], NT, preferred_element_type=F32)

    for c in range(0, HALF, CH):
        got = partial((1 - k) * HALF + c)
        p_snd[:, :, c : c + CH] = got.astype(BF16).reshape(CHIPS, PAIR, CH)
    p_copy = remote(p_snd, p_rcv, s_p.at[0], r_p.at[0], sib)
    p_copy.start()
    for c in range(0, HALF, CH):
        p_own[:, :, c : c + CH] = partial(k * HALF + c).reshape(CHIPS, PAIR, CH)
    for n, up in enumerate(order):
        w_own[n] = grad_share(lax.rem(z + up, NZ), yh)
    p_copy.wait()
    r_copies = []
    for i, o in enumerate(OFFS):
        there = chip(o, 1)
        r_snd[i] = (p_own[there] + p_rcv[there].astype(F32)).astype(BF16)
        cp = remote(r_snd.at[i], r_rcv.at[lax.rem(q, 2), slot], s_r.at[i], r_r.at[i],
                    {"grp": g, "ep": there * 2 + k})
        cp.start()
        r_copies.append(cp)
    r_rcv[lax.rem(q, 2), slot] = (p_own[q] + p_rcv[q].astype(F32)).astype(BF16)

    cand_a = mine[0:1, 0:1]
    cand_b = theirs[0:1, 0:1]

    def both(n):
        y_copies[n].wait_recv()
        a, b = w_own[n].astype(F32), wy_rcv[n].astype(F32)
        return [
            jnp.where(cand_a == c, a, 0.0) + jnp.where(cand_b == c, b, 0.0) for c in (0, 1)
        ]

    def ring(snd, rcv, ssem, rsem, t, n, to, prev):
        terms = both(n)
        if prev is not None:
            prev.wait_recv()
        for c in (0, 1):
            value = terms[c]
            if prev is not None:
                value = value + rcv[t - 1, c].astype(F32)
            snd[t, c] = value.astype(BF16)
        cp = remote(snd.at[t], rcv.at[t], ssem.at[t], rsem.at[t], to)
        cp.start()
        return cp

    downs, ups = [], []
    for t in range(4):
        n = order.index((4 + t) % NZ)
        downs.append(ring(rm_snd, rm_rcv, s_m, r_m, t, n, zdn, downs[-1] if downs else None))
        if t < 3:
            n = order.index(3 - t)
            ups.append(ring(rp_snd, rp_rcv, s_q, r_q, t, n, zup, ups[-1] if ups else None))
    total = both(order.index(0))
    ups[-1].wait_recv()
    total = [total[c] + rp_rcv[2, c].astype(F32) for c in (0, 1)]
    downs[-1].wait_recv()
    total = [total[c] + rm_rcv[3, c].astype(F32) for c in (0, 1)]
    for c in (0, 1):
        grad = total[c]
        first = beta_one * m1v[c] + (1.0 - beta_one) * grad
        second = beta_two * m2v[c] + (1.0 - beta_two) * grad * grad
        m1v[c] = first
        m2v[c] = second
        step = first / first_fix / (jnp.sqrt(second / second_fix) + adam_eps)
        dall[z, c] = step.astype(BF16)
    outs = [
        pltpu.make_async_copy(m1v, nf_out, lsem.at[0]),
        pltpu.make_async_copy(m2v, ns_out, lsem.at[1]),
    ]
    for cp in outs:
        cp.start()

    d_copies = []

    def use(n, zo):
        for buf, cand in ((dy, cand_b), (ds, cand_a)):
            buf[n] = jnp.where(cand == 0, dall[zo, 0].astype(F32), dall[zo, 1].astype(F32)).astype(BF16)
        at = cols(zo * 2 + yh)
        cp = remote(dy.at[n], sd_out.at[0, :, at], s_d.at[n], r_d.at[n], ypart)
        cp.start()
        d_copies.append(cp)
        cp = pltpu.make_async_copy(ds.at[n], sd_out.at[0, :, at], l_d.at[n])
        cp.start()
        outs.append(cp)

    def pass_on(zo, ssem, rsem, t, to):
        cp = remote(dall.at[zo], dall.at[zo], ssem.at[t], rsem.at[t], to)
        cp.start()
        return cp

    a_up = [pass_on(z, s_ap, r_ap, 0, zup)]
    a_dn = [pass_on(z, s_am, r_am, 0, zdn)]
    use(0, z)

    def combine():
        for cp in r_copies:
            cp.wait_recv()
        for c in range(0, HALF, CH):
            got = jnp.zeros((2 * TOK, CH), F32)
            for ab in (0, 1):
                rows = r_rcv[ab, :, :, c : c + CH].reshape(SLOTS * PAIR, CH)
                got += jnp.dot(sel_t[...], rows, preferred_element_type=F32)
            tgv[:, :, c : c + CH] = got.astype(BF16).reshape(2, TOK, CH)
        across = remote(tgv.at[1 - k], tg_out.at[:, mine_cols], s_tg.at[0], r_tg.at[0], sib)
        across.start()
        own = pltpu.make_async_copy(tgv.at[k], tg_out.at[:, mine_cols], lsem.at[2])
        own.start()
        return across, own

    for t in range(4):
        below = lax.rem(z + NZ - t - 1, NZ)
        a_up[t].wait_recv()
        if t < 3:
            a_up.append(pass_on(below, s_ap, r_ap, t + 1, zup))
        use(1 + t, below)
        if t < 3:
            above = lax.rem(z + t + 1, NZ)
            a_dn[t].wait_recv()
            if t < 2:
                a_dn.append(pass_on(above, s_am, r_am, t + 1, zdn))
            use(5 + t, above)
        if t == 1:
            tg_copy, tg_own = combine()

    tg_copy.wait()
    tg_own.wait()
    for cp in d_copies:
        cp.wait()
    for cp in outs:
        cp.wait()
    for cp in y_copies + r_copies + downs + ups + a_up + a_dn:
        cp.wait_send()


def step(tokens, expert_ids, gate_probs, placement, gate_weight, up_weight, down_weight,
         out_grad, moment_first, moment_second):
    def vm(*shape, dtype=BF16):
        return pltpu.VMEM(shape, dtype)

    dma = lambda n: pltpu.SemaphoreType.DMA((n,))
    anywhere = pl.BlockSpec(memory_space=pl.ANY)
    outs = pl.pallas_call(
        body,
        out_shape=(
            jax.ShapeDtypeStruct((TOK, D), BF16),
            jax.ShapeDtypeStruct((1, HU, D), BF16),
            jax.ShapeDtypeStruct((2, HU, SHARE), F32),
            jax.ShapeDtypeStruct((2, HU, SHARE), F32),
        ),
        in_specs=[anywhere] * 3 + [pl.BlockSpec(memory_space=pltpu.SMEM)] + [anywhere] * 6,
        out_specs=(anywhere,) * 4,
        scratch_shapes=[
            vm(2, TOK, HALF), vm(2, TOK, HALF),
            vm(2, TOK, 8, dtype=jnp.int32), vm(2, TOK, 8, dtype=F32),
            vm(2 * TOK, 128, dtype=F32), vm(2 * TOK, 128, dtype=F32),
            vm(2 * TOK, SLOTS * PAIR),
            vm(SLOTS, PAIR, HALF), vm(SLOTS, PAIR, HALF),
            vm(2, CHIPS, PAIR, HALF), vm(2, CHIPS, PAIR, HALF),
            vm(D, HU), vm(D, HU), vm(HU, D),
            vm(2, HU, SHARE, dtype=F32), vm(2, HU, SHARE, dtype=F32),
            vm(HU, ROWS), vm(ROWS, HU), vm(ROWS, HU),
            vm(CHIPS, PAIR, HALF), vm(CHIPS, PAIR, HALF), vm(CHIPS, PAIR, HALF, dtype=F32),
            vm(NO, PAIR, HALF), vm(2, SLOTS, PAIR, HALF), vm(2, TOK, HALF),
            vm(8, 128, dtype=jnp.int32), vm(8, 128, dtype=jnp.int32),
            vm(NZ, HU, SHARE), vm(NZ, HU, SHARE), vm(NZ, HU, SHARE),
            vm(4, 2, HU, SHARE), vm(4, 2, HU, SHARE), vm(3, 2, HU, SHARE), vm(3, 2, HU, SHARE),
            vm(NZ, 2, HU, SHARE), vm(NZ, HU, SHARE), vm(NZ, HU, SHARE),
            dma(9), dma(4), dma(4),
            dma(8), dma(8), dma(8), dma(8), dma(8), dma(8), dma(8), dma(8),
            dma(1), dma(1), dma(8), dma(8), dma(1), dma(1),
            dma(1), dma(1), dma(8), dma(8), dma(4), dma(4), dma(4), dma(4),
            dma(4), dma(4), dma(4), dma(4), dma(8), dma(8), dma(8),
        ],
        compiler_params=pltpu.CompilerParams(
            collective_id=0, has_side_effects=True, vmem_limit_bytes=60 * 2**20
        ),
    )(tokens, expert_ids, gate_probs, placement, gate_weight, up_weight, down_weight,
      out_grad, moment_first, moment_second)
    return outs


def solution(mesh):
    return jax.shard_map(
        step,
        mesh=mesh,
        in_specs=(
            P(("grp", "ep"), None),
            P(("grp", "ep"), None),
            P(("grp", "ep"), None),
            P("grp", None),
            P("grp", None, "ep"),
            P("grp", None, "ep"),
            P("grp", "ep", None),
            P(("grp", "ep"), None),
            P(None, "ep", "grp"),
            P(None, "ep", "grp"),
        ),
        out_specs=(
            P(("grp", "ep"), None),
            P("grp", "ep", None),
            P(None, "ep", "grp"),
            P(None, "ep", "grp"),
        ),
        check_vma=False,
    )
```

```python
import math

import jax
import jax.numpy as jnp
from jax import lax
from jax.experimental import pallas as pl
from jax.experimental.pallas import tpu as pltpu
from jax.sharding import PartitionSpec as P

MESH = pl.DeviceIdType.MESH
F32 = jnp.float32
BF16 = jnp.bfloat16

D = 4096
HALF = 2048
TOK = 192
HU = 192
CAP = 24
PAIR = 2 * CAP
SLOTS = 4
CHIPS = 8
NX = 4
NZ = 8
SHARE = 256
ROWS = CHIPS * PAIR
CH = 512

beta_one = 0.9
beta_two = 0.999
adam_eps = 1e-08
first_fix = 1.0 - math.exp(1000.0 * math.log(0.9))
second_fix = 1.0 - math.exp(1000.0 * math.log(0.999))

XD = (2, 1, 3)
NC = 4
NT = (((1,), (1,)), ((), ()))


def body(
    tok, ids, prb, plc, wg, wu, wd, og, m1, m2,
    tg_out, sd_out, nf_out, ns_out,
    tokH, grdH, idsH, prbH, sel_t, snd_t, snd_g, rel_t, rel_g, xt, xg,
    wgv, wuv, wdv, m1v, m2v, hid_t, dgv, duv,
    p_snd, p_rcv, p_own, r_snd, fin, relr, rel_s, rback, tgv,
    mine, theirs, wy_snd, wy_rcv, w_own,
    rm_snd, rm_rcv, rp_snd, rp_rcv, dall, dy,
    lsem, s_in, r_in,
    tl, tys, tyr, txs, txr, tfs, tfr, gl, gys, gyr, gxs, gxr, gfs, gfr,
    s_p, r_p, s_r, r_r, s_ry, r_ry, s_tg, r_tg,
    s_c, r_c, s_y, r_y, s_m, r_m, s_q, r_q, s_am, r_am, s_ap, r_ap, s_d, r_d,
):
    g = lax.axis_index("grp")
    e = lax.axis_index("ep")
    z, yh = g // 2, lax.rem(g, 2)
    q, k = e // 2, lax.rem(e, 2)
    yl, x = q // NX, lax.rem(q, NX)
    slot = q // 2
    row_slots, far_slots = yl * 2, (1 - yl) * 2
    side = x // 2
    q_far = (1 - yl) * NX + x
    sib = {"grp": g, "ep": q * 2 + 1 - k}
    far = {"grp": g, "ep": q_far * 2 + k}
    ypart = {"grp": z * 2 + 1 - yh, "ep": e}
    zup = {"grp": lax.rem(z + 1, NZ) * 2 + yh, "ep": e}
    zdn = {"grp": lax.rem(z + NZ - 1, NZ) * 2 + yh, "ep": e}
    x_of = [lax.rem(x + d, NX) for d in XD]
    x_from = [lax.rem(x - d + NX, NX) for d in XD]
    along = [{"grp": g, "ep": (yl * NX + xd) * 2 + k} for xd in x_of]

    def remote(src, dst, ssem, rsem, to):
        return pltpu.make_async_remote_copy(
            src_ref=src, dst_ref=dst, send_sem=ssem, recv_sem=rsem, device_id=to,
            device_id_type=MESH,
        )

    def cols(i):
        return pl.ds(pl.multiple_of(i * SHARE, SHARE), SHARE)

    mine_cols = pl.ds(pl.multiple_of(k * HALF, HALF), HALF)
    other_cols = pl.ds(pl.multiple_of((1 - k) * HALF, HALF), HALF)

    local = [
        pltpu.make_async_copy(ids, idsH.at[k], lsem.at[0]),
        pltpu.make_async_copy(prb, prbH.at[k], lsem.at[1]),
        pltpu.make_async_copy(tok.at[:, mine_cols], tokH.at[k], lsem.at[2]),
        pltpu.make_async_copy(og.at[:, mine_cols], grdH.at[k], lsem.at[3]),
    ]
    later = [
        pltpu.make_async_copy(wg.at[0], wgv, lsem.at[4]),
        pltpu.make_async_copy(wu.at[0], wuv, lsem.at[5]),
        pltpu.make_async_copy(wd.at[0], wdv, lsem.at[6]),
        pltpu.make_async_copy(m1, m1v, lsem.at[7]),
        pltpu.make_async_copy(m2, m2v, lsem.at[8]),
    ]
    for cp in local:
        cp.start()
    mine[...] = jnp.zeros((8, 128), jnp.int32) + plc[0, slot]

    barrier = pltpu.get_barrier_semaphore()
    greet = [sib, far, ypart, zup, zdn] + along
    for to in greet:
        pl.semaphore_signal(barrier, inc=1, device_id=to, device_id_type=MESH)
    pl.semaphore_wait(barrier, len(greet))

    swap = [
        remote(ids, idsH.at[k], s_in.at[0], r_in.at[0], sib),
        remote(prb, prbH.at[k], s_in.at[1], r_in.at[1], sib),
        remote(tok.at[:, other_cols], tokH.at[k], s_in.at[2], r_in.at[2], sib),
        remote(og.at[:, other_cols], grdH.at[k], s_in.at[3], r_in.at[3], sib),
    ]
    for cp in swap:
        cp.start()
    cand_copy = remote(mine, theirs, s_c.at[0], r_c.at[0], ypart)
    cand_copy.start()
    for cp in later:
        cp.start()

    for i in (0, 1):
        local[i].wait()
        swap[i].wait()
    row = lax.broadcasted_iota(jnp.int32, (TOK, TOK), 0)
    col = lax.broadcasted_iota(jnp.int32, (TOK, TOK), 1)
    before = jnp.where(row < col, 1.0, 0.0).astype(BF16)
    line = lax.broadcasted_iota(jnp.int32, (8, TOK), 0)
    r48 = lax.broadcasted_iota(jnp.int32, (PAIR, TOK), 0)
    place = jnp.where(r48 >= CAP, r48 - CAP, r48).astype(F32)
    pick_all = []
    scale_all = jnp.zeros((SLOTS * PAIR, 1), F32)
    for kk in (0, 1):
        id_rows, prob_rows = idsH[kk], prbH[kk]
        hits = jnp.zeros((8, TOK), F32)
        coefs = []
        for s in range(SLOTS):
            match = id_rows == plc[0, s] * SLOTS + s
            hit = jnp.max(jnp.where(match, 1.0, 0.0), axis=0, keepdims=True)
            coefs.append(jnp.sum(jnp.where(match, prob_rows, 0.0), axis=0, keepdims=True))
            hits = jnp.where(line == s, hit, hits)
        rank = jnp.dot(hits.astype(BF16), before, preferred_element_type=F32)
        own_rows = (r48 >= CAP) == (kk == 1)
        picks, scales = [], []
        for s in range(SLOTS):
            ok = own_rows & (hits[s : s + 1] > 0.5) & (rank[s : s + 1] == place)
            pick = jnp.where(ok, 1.0, 0.0)
            picks.append(pick)
            scales.append(jnp.sum(pick * coefs[s], axis=1, keepdims=True))
        pick = jnp.concatenate(picks, axis=0)
        scale_all += jnp.concatenate(scales, axis=0)
        sel_t[kk] = jnp.transpose(pick).astype(BF16)
        pick_all.append(pick.astype(BF16))

    def select(src, c):
        at = slice(c * CH, (c + 1) * CH)
        got = jnp.dot(pick_all[0], src[0, :, at], preferred_element_type=F32)
        return got + jnp.dot(pick_all[1], src[1, :, at], preferred_element_type=F32)

    class Route:
        def __init__(self, block, land, relay, sems, nth):
            ls, ys, yr, xs, xr, fs, fr = sems
            self.own = pltpu.make_async_copy(
                block(row_slots + side), land(q), ls.at[2 * nth]
            )
            self.own_far = pltpu.make_async_copy(
                relay(side), land(q_far), ls.at[2 * nth + 1]
            )
            self.y = [
                remote(block(far_slots + p), relay(p), ys.at[2 * nth + p], yr.at[2 * nth + p], far)
                for p in (0, 1)
            ]
            self.x_near, self.x_far = [], []
            for i in range(3):
                there, at = x_of[i] // 2, 6 * nth + i
                self.x_near.append(remote(block(row_slots + there), land(q),
                                          xs.at[at], xr.at[at], along[i]))
                self.x_far.append(remote(relay(there), land(q_far),
                                         xs.at[at + 3], xr.at[at + 3], along[i]))
            at = 8 * nth
            self.f_own = remote(block(row_slots + side), land(q), fs.at[at], fr.at[at], sib)
            self.f_far = remote(relay(side), land(q_far), fs.at[at + 1], fr.at[at + 1], sib)
            self.f_near_x, self.f_far_x = [], []
            for i in range(3):
                for kept, base, off in (
                    (self.f_near_x, yl * NX, 2), (self.f_far_x, (1 - yl) * NX, 5)
                ):
                    ref = land(base + x_from[i])
                    kept.append(remote(ref, ref, fs.at[at + off + i], fr.at[at + off + i], sib))

        def start_y(self):
            for cp in self.y:
                cp.start()

        def start_near(self):
            for cp in self.x_near:
                cp.start()
            self.own.start()
            self.f_own.start()

        def start_far(self):
            for cp in self.y:
                cp.wait_recv()
            for cp in self.x_far:
                cp.start()
            self.own_far.start()
            self.f_far.start()

        def arrive(self):
            for i in (1, 2, 0):
                self.x_near[i].wait_recv()
                self.f_near_x[i].start()
            for i in (1, 2, 0):
                self.x_far[i].wait_recv()
                self.f_far_x[i].start()
            for cp in [self.f_own, self.f_far] + self.f_near_x + self.f_far_x:
                cp.wait()
            self.own.wait()
            self.own_far.wait()

        def end(self):
            for cp in self.y + self.x_near + self.x_far:
                cp.wait_send()

    toks = Route(
        lambda s: snd_t.at[s], lambda c: xt.at[k, c], lambda p: rel_t.at[p],
        (tl, tys, tyr, txs, txr, tfs, tfr), 0,
    )
    chunk_of = [lax.rem(z + o, NC) for o in (0, 3, 1, 2)]

    def grad_route(n):
        c = chunk_of[n]
        return Route(
            lambda s: snd_g.at[c, s], lambda chip: xg.at[k, c, chip], lambda p: rel_g.at[n, p],
            (gl, gys, gyr, gxs, gxr, gfs, gfr), n,
        )

    grads = [grad_route(n) for n in range(NC)]

    local[2].wait()
    swap[2].wait()
    for c in range(NC):
        got = select(tokH, c)
        snd_t[:, :, c * CH : (c + 1) * CH] = got.astype(BF16).reshape(SLOTS, PAIR, CH)
    toks.start_y()
    toks.start_near()
    local[3].wait()
    swap[3].wait()
    for c in range(NC):
        got = select(grdH, c) * scale_all
        snd_g[c] = got.astype(BF16).reshape(SLOTS, PAIR, CH)
    toks.start_far()
    for r in grads:
        r.start_y()
    for n in range(NC):
        grads[n].start_near()
        grads[n].start_far()
    for cp in later:
        cp.wait()
    cand_copy.wait()

    toks.arrive()
    pre_gate = jnp.zeros((ROWS, HU), F32)
    pre_up = jnp.zeros((ROWS, HU), F32)
    for c in range(0, D, CH):
        rows = xt[c // HALF, :, :, c % HALF : c % HALF + CH].reshape(ROWS, CH)
        pre_gate += lax.dot_general(rows, wgv[:, c : c + CH], NT, preferred_element_type=F32)
        pre_up += lax.dot_general(rows, wuv[:, c : c + CH], NT, preferred_element_type=F32)
    sig = jax.nn.sigmoid(pre_gate)
    act = pre_gate * sig
    hid_t[...] = jnp.transpose(act * pre_up).astype(BF16)

    def grad_share(zd, yd):
        at = pl.ds(pl.multiple_of(yd * SHARE, SHARE), SHARE)
        rows = xg[zd // NC, lax.rem(zd, NC), :, :, at].reshape(ROWS, SHARE)
        return jnp.dot(hid_t[...], rows, preferred_element_type=F32).astype(BF16)

    y_copies = [
        remote(wy_snd.at[n], wy_rcv.at[n], s_y.at[n], r_y.at[n], ypart) for n in range(NZ)
    ]

    def shares(pair):
        for n in pair:
            wy_snd[n] = grad_share(lax.rem(z + n, NZ), 1 - yh)
            y_copies[n].start()
        for n in pair:
            w_own[n] = grad_share(lax.rem(z + n, NZ), yh)

    cand_a = mine[0:1, 0:1]
    cand_b = theirs[0:1, 0:1]

    def term(n, c):
        a, b = w_own[n].astype(F32), wy_rcv[n].astype(F32)
        return jnp.where(cand_a == c, a, 0.0) + jnp.where(cand_b == c, b, 0.0)

    def hops(snd, rcv, ssem, rsem, count, to):
        return [
            [
                remote(snd.at[t, c], rcv.at[t, c], ssem.at[2 * t + c], rsem.at[2 * t + c], to)
                for c in (0, 1)
            ]
            for t in range(count)
        ]

    downs = hops(rm_snd, rm_rcv, s_m, r_m, 4, zdn)
    ups = hops(rp_snd, rp_rcv, s_q, r_q, 3, zup)

    def ring(ring_hops, snd, rcv, t, n):
        y_copies[n].wait_recv()
        for c in (0, 1):
            value = term(n, c)
            if t > 0:
                ring_hops[t - 1][c].wait_recv()
                value = value + rcv[t - 1, c].astype(F32)
            snd[t, c] = value.astype(BF16)
            ring_hops[t][c].start()

    down = lambda t: ring(downs, rm_snd, rm_rcv, t, 4 + t)
    up = lambda t: ring(ups, rp_snd, rp_rcv, t, 3 - t)

    grads[0].arrive()
    shares((4, 0))
    grads[1].arrive()
    shares((3, 7))
    down(0)
    grads[2].arrive()
    shares((5, 1))
    up(0)
    grads[3].arrive()
    shares((6, 2))
    down(1)

    d_hidden = jnp.zeros((ROWS, HU), F32)
    for c in range(D // CH):
        rows = xg[c // NC, c % NC].reshape(ROWS, CH)
        d_hidden += lax.dot_general(
            rows, wdv[:, c * CH : (c + 1) * CH], NT, preferred_element_type=F32
        )
    dgv[...] = (d_hidden * pre_up * sig * (1.0 + pre_gate * (1.0 - sig))).astype(BF16)
    duv[...] = (d_hidden * act).astype(BF16)
    up(1)
    down(2)

    def partial(start):
        at = pl.ds(pl.multiple_of(start, CH), CH)
        got = jnp.dot(dgv[...], wgv[:, at], preferred_element_type=F32)
        return got + jnp.dot(duv[...], wuv[:, at], preferred_element_type=F32)

    for c in range(0, HALF, CH):
        got = partial((1 - k) * HALF + c)
        p_snd[:, :, c : c + CH] = got.astype(BF16).reshape(CHIPS, PAIR, CH)
    p_copy = remote(p_snd, p_rcv, s_p.at[0], r_p.at[0], sib)
    p_copy.start()
    up(2)
    down(3)
    for c in range(0, HALF, CH):
        p_own[:, :, c : c + CH] = partial(k * HALF + c).reshape(CHIPS, PAIR, CH)
    p_copy.wait()

    def both_cores(chip):
        return (p_own[chip] + p_rcv[chip].astype(F32)).astype(BF16)

    r_copies = []
    for i in range(3):
        for j, (base, dst) in enumerate((((1 - yl) * NX, relr), (yl * NX, fin))):
            at = 2 * i + j
            r_snd[at] = both_cores(base + x_of[i])
            cp = remote(r_snd.at[at], dst.at[x], s_r.at[at], r_r.at[at], along[i])
            cp.start()
            r_copies.append(cp)
    relr[x] = both_cores(q_far)
    fin[x] = both_cores(q)

    y_copies[0].wait_recv()
    total = [term(0, c) for c in (0, 1)]
    for c in (0, 1):
        ups[-1][c].wait_recv()
        downs[-1][c].wait_recv()
        grad = total[c] + rp_rcv[2, c].astype(F32) + rm_rcv[3, c].astype(F32)
        first = beta_one * m1v[c] + (1.0 - beta_one) * grad
        second = beta_two * m2v[c] + (1.0 - beta_two) * grad * grad
        nf_out[c] = first
        ns_out[c] = second
        step = first / first_fix / (jnp.sqrt(second / second_fix) + adam_eps)
        dall[z, c] = step.astype(BF16)

    d_copies = []

    def use(n, zo):
        at = cols(zo * 2 + yh)
        first, second = dall[zo, 0].astype(F32), dall[zo, 1].astype(F32)
        dy[n] = jnp.where(cand_b == 0, first, second).astype(BF16)
        cp = remote(dy.at[n], sd_out.at[0, :, at], s_d.at[n], r_d.at[n], ypart)
        cp.start()
        d_copies.append(cp)
        sd_out[0, :, at] = jnp.where(cand_a == 0, first, second).astype(BF16)

    def passes(zo, ssem, rsem, t, to):
        return [
            remote(dall.at[zo, c], dall.at[zo, c], ssem.at[2 * t + c], rsem.at[2 * t + c], to)
            for c in (0, 1)
        ]

    below = [lax.rem(z + NZ - t, NZ) for t in range(5)]
    above = [lax.rem(z + t, NZ) for t in range(4)]
    a_up = [passes(below[t], s_ap, r_ap, t, zup) for t in range(4)]
    a_dn = [passes(above[t], s_am, r_am, t, zdn) for t in range(3)]
    for c in (0, 1):
        a_up[0][c].start()
        a_dn[0][c].start()
    use(0, z)

    def relay_back():
        for cp in r_copies:
            cp.wait_recv()
        sent = []
        for p in (0, 1):
            got = relr[2 * p].astype(F32) + relr[2 * p + 1].astype(F32)
            rel_s[p] = got.astype(BF16)
            cp = remote(rel_s.at[p], rback.at[row_slots + p], s_ry.at[p], r_ry.at[p], far)
            cp.start()
            sent.append(cp)
        for p in (0, 1):
            got = fin[2 * p].astype(F32) + fin[2 * p + 1].astype(F32)
            rback[row_slots + p] = got.astype(BF16)
        return sent

    def combine():
        for cp in far_copies:
            cp.wait_recv()
        for c in range(0, HALF, CH):
            rows = rback[:, :, c : c + CH].reshape(SLOTS * PAIR, CH)
            for kk in (0, 1):
                got = jnp.dot(sel_t[kk], rows, preferred_element_type=F32)
                tgv[kk, :, c : c + CH] = got.astype(BF16)
        across = remote(tgv.at[1 - k], tg_out.at[:, mine_cols], s_tg.at[0], r_tg.at[0], sib)
        across.start()
        tg_out[:, mine_cols] = tgv[k]
        return across

    for t in range(4):
        for c in (0, 1):
            a_up[t][c].wait_recv()
            if t < 3:
                a_up[t + 1][c].start()
            if t < 3:
                a_dn[t][c].wait_recv()
                if t < 2:
                    a_dn[t + 1][c].start()
        use(1 + t, below[t + 1])
        if t < 3:
            use(5 + t, above[t + 1])
        if t == 1:
            far_copies = relay_back()
        if t == 2:
            tg_copy = combine()

    tg_copy.wait()
    for cp in d_copies:
        cp.wait()
    for r in [toks] + grads:
        r.end()
    for cp in y_copies + r_copies + far_copies:
        cp.wait_send()
    for hop in downs + ups + a_up + a_dn:
        for cp in hop:
            cp.wait_send()


def step(tokens, expert_ids, gate_probs, placement, gate_weight, up_weight, down_weight,
         out_grad, moment_first, moment_second):
    def vm(*shape, dtype=BF16):
        return pltpu.VMEM(shape, dtype)

    dma = lambda n: pltpu.SemaphoreType.DMA((n,))
    anywhere = pl.BlockSpec(memory_space=pl.ANY)
    outs = pl.pallas_call(
        body,
        out_shape=(
            vm(TOK, D), vm(1, HU, D), vm(2, HU, SHARE, dtype=F32), vm(2, HU, SHARE, dtype=F32),
        ),
        in_specs=[anywhere] * 3 + [pl.BlockSpec(memory_space=pltpu.SMEM)] + [anywhere] * 6,
        out_specs=(pl.BlockSpec(memory_space=pltpu.VMEM),) * 4,
        scratch_shapes=[
            vm(2, TOK, HALF), vm(2, TOK, HALF),
            vm(2, 8, TOK, dtype=jnp.int32), vm(2, 8, TOK, dtype=F32),
            vm(2, TOK, SLOTS * PAIR),
            vm(SLOTS, PAIR, HALF), vm(NC, SLOTS, PAIR, CH),
            vm(2, PAIR, HALF), vm(NC, 2, PAIR, CH),
            vm(2, CHIPS, PAIR, HALF), vm(2, NC, CHIPS, PAIR, CH),
            vm(HU, D), vm(HU, D), vm(HU, D),
            vm(2, HU, SHARE, dtype=F32), vm(2, HU, SHARE, dtype=F32),
            vm(HU, ROWS), vm(ROWS, HU), vm(ROWS, HU),
            vm(CHIPS, PAIR, HALF), vm(CHIPS, PAIR, HALF), vm(CHIPS, PAIR, HALF, dtype=F32),
            vm(6, PAIR, HALF), vm(NX, PAIR, HALF), vm(NX, PAIR, HALF),
            vm(2, PAIR, HALF), vm(SLOTS, PAIR, HALF), vm(2, TOK, HALF),
            vm(8, 128, dtype=jnp.int32), vm(8, 128, dtype=jnp.int32),
            vm(NZ, HU, SHARE), vm(NZ, HU, SHARE), vm(NZ, HU, SHARE),
            vm(4, 2, HU, SHARE), vm(4, 2, HU, SHARE), vm(3, 2, HU, SHARE), vm(3, 2, HU, SHARE),
            vm(NZ, 2, HU, SHARE), vm(NZ, HU, SHARE),
            dma(9), dma(4), dma(4),
            dma(2), dma(2), dma(2), dma(6), dma(6), dma(8), dma(8),
            dma(2 * NC), dma(2 * NC), dma(2 * NC), dma(6 * NC), dma(6 * NC), dma(8 * NC),
            dma(8 * NC),
            dma(1), dma(1), dma(6), dma(6), dma(2), dma(2), dma(1), dma(1),
            dma(1), dma(1), dma(8), dma(8), dma(8), dma(8), dma(6), dma(6),
            dma(6), dma(6), dma(8), dma(8), dma(8), dma(8),
        ],
        compiler_params=pltpu.CompilerParams(
            collective_id=0, has_side_effects=True, vmem_limit_bytes=60 * 2**20
        ),
    )(tokens, expert_ids.T, gate_probs.T, placement, jnp.swapaxes(gate_weight, 1, 2),
      jnp.swapaxes(up_weight, 1, 2), down_weight, out_grad, moment_first, moment_second)
    return outs


def solution(mesh):
    return jax.shard_map(
        step,
        mesh=mesh,
        in_specs=(
            P(("grp", "ep"), None),
            P(("grp", "ep"), None),
            P(("grp", "ep"), None),
            P("grp", None),
            P("grp", None, "ep"),
            P("grp", None, "ep"),
            P("grp", "ep", None),
            P(("grp", "ep"), None),
            P(None, "ep", "grp"),
            P(None, "ep", "grp"),
        ),
        out_specs=(
            P(("grp", "ep"), None),
            P("grp", "ep", None),
            P(None, "ep", "grp"),
            P(None, "ep", "grp"),
        ),
        check_vma=False,
    )
```

```python
import math

import jax
import jax.numpy as jnp
from jax import lax
from jax.experimental import pallas as pl
from jax.experimental.pallas import tpu as pltpu
from jax.sharding import PartitionSpec as P

MESH = pl.DeviceIdType.MESH
F32 = jnp.float32
BF16 = jnp.bfloat16

D = 4096
HALF = 2048
TOK = 192
HU = 192
CAP = 24
PAIR = 2 * CAP
SLOTS = 4
CHIPS = 8
NX = 4
NZ = 8
SHARE = 256
ROWS = CHIPS * PAIR
CH = 512

beta_one = 0.9
beta_two = 0.999
adam_eps = 1e-08
first_fix = 1.0 - math.exp(1000.0 * math.log(0.9))
second_fix = 1.0 - math.exp(1000.0 * math.log(0.999))

XD = (2, 1, 3)
NC = 4
NR = 2
PIECE = HU // NR
CHUNKS = ((4, 0), (3, 5), (2, 6), (1, 7))
NT = (((1,), (1,)), ((), ()))


def body(
    tok, ids, prb, plc, wg, wu, wd, og, m1, m2,
    tg_out, sd_out, nf_out, ns_out,
    tokH, grdH, idsH, prbH, sel_t, snd_t, snd_g, rel_t, rel_g, xt, xg,
    wgv, wuv, wdv, m1v, m2v, hid_t, dhv, dgv, duv,
    p_snd, p_rcv, p_own, r_snd, fin, relr, rel_s, rback, tgv,
    mine, theirs, wy_snd, wy_rcv, w_own,
    rm_snd, rm_rcv, rp_snd, rp_rcv, dall, dy,
    lsem, s_in, r_in,
    tl, tys, tyr, txs, txr, tfs, tfr, gl, gys, gyr, gxs, gxr, gfs, gfr,
    s_p, r_p, s_r, r_r, s_ry, r_ry, s_tg, r_tg,
    s_c, r_c, s_y, r_y, s_m, r_m, s_q, r_q, s_am, r_am, s_ap, r_ap, s_d, r_d,
):
    g = lax.axis_index("grp")
    e = lax.axis_index("ep")
    z, yh = g // 2, lax.rem(g, 2)
    q, k = e // 2, lax.rem(e, 2)
    yl, x = q // NX, lax.rem(q, NX)
    slot = q // 2
    row_slots, far_slots = yl * 2, (1 - yl) * 2
    side = x // 2
    q_far = (1 - yl) * NX + x
    sib = {"grp": g, "ep": q * 2 + 1 - k}
    far = {"grp": g, "ep": q_far * 2 + k}
    ypart = {"grp": z * 2 + 1 - yh, "ep": e}
    zup = {"grp": lax.rem(z + 1, NZ) * 2 + yh, "ep": e}
    zdn = {"grp": lax.rem(z + NZ - 1, NZ) * 2 + yh, "ep": e}
    x_of = [lax.rem(x + d, NX) for d in XD]
    x_from = [lax.rem(x - d + NX, NX) for d in XD]
    along = [{"grp": g, "ep": (yl * NX + xd) * 2 + k} for xd in x_of]

    def remote(src, dst, ssem, rsem, to):
        return pltpu.make_async_remote_copy(
            src_ref=src, dst_ref=dst, send_sem=ssem, recv_sem=rsem, device_id=to,
            device_id_type=MESH,
        )

    def cols(i):
        return pl.ds(pl.multiple_of(i * SHARE, SHARE), SHARE)

    mine_cols = pl.ds(pl.multiple_of(k * HALF, HALF), HALF)
    other_cols = pl.ds(pl.multiple_of((1 - k) * HALF, HALF), HALF)

    local = [
        pltpu.make_async_copy(ids, idsH.at[k], lsem.at[0]),
        pltpu.make_async_copy(prb, prbH.at[k], lsem.at[1]),
        pltpu.make_async_copy(tok.at[:, mine_cols], tokH.at[k], lsem.at[2]),
    ]
    local_g = [
        pltpu.make_async_copy(og.at[:, cols(2 * i + k)], grdH.at[k, i], lsem.at[8 + i])
        for i in range(NZ)
    ]
    later = [
        pltpu.make_async_copy(wg.at[0], wgv, lsem.at[3]),
        pltpu.make_async_copy(wu.at[0], wuv, lsem.at[4]),
        pltpu.make_async_copy(wd.at[0], wdv, lsem.at[5]),
        pltpu.make_async_copy(m1, m1v, lsem.at[6]),
        pltpu.make_async_copy(m2, m2v, lsem.at[7]),
    ]
    for cp in local + local_g:
        cp.start()
    mine[...] = jnp.zeros((8, 128), jnp.int32) + plc[0, slot]

    barrier = pltpu.get_barrier_semaphore()
    greet = [sib, far, ypart, zup, zdn] + along
    for to in greet:
        pl.semaphore_signal(barrier, inc=1, device_id=to, device_id_type=MESH)
    pl.semaphore_wait(barrier, len(greet))

    swap = [
        remote(ids, idsH.at[k], s_in.at[0], r_in.at[0], sib),
        remote(prb, prbH.at[k], s_in.at[1], r_in.at[1], sib),
        remote(tok.at[:, other_cols], tokH.at[k], s_in.at[2], r_in.at[2], sib),
    ]
    swap_g = [
        remote(og.at[:, cols(2 * i + 1 - k)], grdH.at[k, i], s_in.at[3 + i], r_in.at[3 + i], sib)
        for i in range(NZ)
    ]
    for cp in swap + swap_g:
        cp.start()
    cand_copy = remote(mine, theirs, s_c.at[0], r_c.at[0], ypart)
    cand_copy.start()
    for cp in later:
        cp.start()

    for i in (0, 1):
        local[i].wait()
        swap[i].wait()
    row = lax.broadcasted_iota(jnp.int32, (TOK, TOK), 0)
    col = lax.broadcasted_iota(jnp.int32, (TOK, TOK), 1)
    before = jnp.where(row < col, 1.0, 0.0).astype(BF16)
    line = lax.broadcasted_iota(jnp.int32, (8, TOK), 0)
    r48 = lax.broadcasted_iota(jnp.int32, (PAIR, TOK), 0)
    place = jnp.where(r48 >= CAP, r48 - CAP, r48).astype(F32)
    pick_all = []
    scale_all = jnp.zeros((SLOTS * PAIR, 1), F32)
    for kk in (0, 1):
        id_rows, prob_rows = idsH[kk], prbH[kk]
        hits = jnp.zeros((8, TOK), F32)
        coefs = []
        for s in range(SLOTS):
            match = id_rows == plc[0, s] * SLOTS + s
            hit = jnp.max(jnp.where(match, 1.0, 0.0), axis=0, keepdims=True)
            coefs.append(jnp.sum(jnp.where(match, prob_rows, 0.0), axis=0, keepdims=True))
            hits = jnp.where(line == s, hit, hits)
        rank = jnp.dot(hits.astype(BF16), before, preferred_element_type=F32)
        own_rows = (r48 >= CAP) == (kk == 1)
        picks, scales = [], []
        for s in range(SLOTS):
            ok = own_rows & (hits[s : s + 1] > 0.5) & (rank[s : s + 1] == place)
            pick = jnp.where(ok, 1.0, 0.0)
            picks.append(pick)
            scales.append(jnp.sum(pick * coefs[s], axis=1, keepdims=True))
        pick = jnp.concatenate(picks, axis=0)
        scale_all += jnp.concatenate(scales, axis=0)
        sel_t[kk] = jnp.transpose(pick).astype(BF16)
        pick_all.append(pick.astype(BF16))

    def select(rows_a, rows_b):
        got = jnp.dot(pick_all[0], rows_a, preferred_element_type=F32)
        return got + jnp.dot(pick_all[1], rows_b, preferred_element_type=F32)

    class Route:
        def __init__(self, block, land, relay, sems, nth):
            ls, ys, yr, xs, xr, fs, fr = sems
            self.own = pltpu.make_async_copy(
                block(row_slots + side), land(q), ls.at[2 * nth]
            )
            self.own_far = pltpu.make_async_copy(
                relay(side), land(q_far), ls.at[2 * nth + 1]
            )
            self.y = [
                remote(block(far_slots + p), relay(p), ys.at[2 * nth + p], yr.at[2 * nth + p], far)
                for p in (0, 1)
            ]
            self.x_near, self.x_far = [], []
            for i in range(3):
                there, at = x_of[i] // 2, 6 * nth + i
                self.x_near.append(remote(block(row_slots + there), land(q),
                                          xs.at[at], xr.at[at], along[i]))
                self.x_far.append(remote(relay(there), land(q_far),
                                         xs.at[at + 3], xr.at[at + 3], along[i]))
            at = 8 * nth
            self.f_own = remote(block(row_slots + side), land(q), fs.at[at], fr.at[at], sib)
            self.f_far = remote(relay(side), land(q_far), fs.at[at + 1], fr.at[at + 1], sib)
            self.f_near_x, self.f_far_x = [], []
            for i in range(3):
                for kept, base, off in (
                    (self.f_near_x, yl * NX, 2), (self.f_far_x, (1 - yl) * NX, 5)
                ):
                    ref = land(base + x_from[i])
                    kept.append(remote(ref, ref, fs.at[at + off + i], fr.at[at + off + i], sib))

        def start_y(self):
            for cp in self.y:
                cp.start()

        def start_near(self):
            for cp in self.x_near:
                cp.start()
            self.own.start()
            self.f_own.start()

        def start_far(self):
            for cp in self.y:
                cp.wait_recv()
            for cp in self.x_far:
                cp.start()
            self.own_far.start()
            self.f_far.start()

        def arrive(self):
            for i in (1, 2, 0):
                self.x_near[i].wait_recv()
                self.f_near_x[i].start()
            for i in (1, 2, 0):
                self.x_far[i].wait_recv()
                self.f_far_x[i].start()
            for cp in [self.f_own, self.f_far] + self.f_near_x + self.f_far_x:
                cp.wait()
            self.own.wait()
            self.own_far.wait()

        def end(self):
            for cp in self.y + self.x_near + self.x_far:
                cp.wait_send()

    toks = Route(
        lambda s: snd_t.at[s], lambda c: xt.at[k, c], lambda p: rel_t.at[p],
        (tl, tys, tyr, txs, txr, tfs, tfr), 0,
    )
    owner = [lax.rem(z + n, NZ) for n in range(NZ)]

    def grad_route(n):
        return Route(
            lambda s: snd_g.at[n, s], lambda chip: xg.at[k, n, chip], lambda p: rel_g.at[n, p],
            (gl, gys, gyr, gxs, gxr, gfs, gfr), n,
        )

    grads = [grad_route(n) for n in range(NC)]

    local[2].wait()
    swap[2].wait()
    for c in range(NC):
        at = slice(c * CH, (c + 1) * CH)
        got = select(tokH[0, :, at], tokH[1, :, at])
        snd_t[:, :, at] = got.astype(BF16).reshape(SLOTS, PAIR, CH)
    toks.start_y()
    toks.start_near()
    for cp in local_g + swap_g:
        cp.wait()
    for c, pair in enumerate(CHUNKS):
        for j, n in enumerate(pair):
            got = select(grdH[0, owner[n]], grdH[1, owner[n]]) * scale_all
            at = slice(j * SHARE, (j + 1) * SHARE)
            snd_g[c, :, :, at] = got.astype(BF16).reshape(SLOTS, PAIR, SHARE)
    for r in grads:
        r.start_y()
    grads[0].start_near()
    toks.start_far()
    grads[0].start_far()
    for n in range(1, NC):
        grads[n].start_near()
        grads[n].start_far()
    for cp in later:
        cp.wait()
    cand_copy.wait()

    toks.arrive()
    pre_gate = jnp.zeros((ROWS, HU), F32)
    pre_up = jnp.zeros((ROWS, HU), F32)
    for c in range(0, D, CH):
        rows = xt[c // HALF, :, :, c % HALF : c % HALF + CH].reshape(ROWS, CH)
        pre_gate += lax.dot_general(rows, wgv[:, c : c + CH], NT, preferred_element_type=F32)
        pre_up += lax.dot_general(rows, wuv[:, c : c + CH], NT, preferred_element_type=F32)
    sig = jax.nn.sigmoid(pre_gate)
    act = pre_gate * sig
    hid_t[...] = jnp.transpose(act * pre_up).astype(BF16)

    def rows_of(n, yd):
        [(c, j)] = [(c, pair.index(n)) for c, pair in enumerate(CHUNKS) if n in pair]
        return xg[yd, c, :, :, j * SHARE : (j + 1) * SHARE].reshape(ROWS, SHARE)

    def grad_share(n, yd):
        got = jnp.dot(hid_t[...], rows_of(n, yd), preferred_element_type=F32)
        return got.astype(BF16).reshape(NR, PIECE, SHARE)

    def pieces(n, make):
        return [make(n, r, NR * n + r) for r in range(NR)]

    y_copies = [
        pieces(n, lambda n, r, i: remote(wy_snd.at[n, r], wy_rcv.at[n, r], s_y.at[i], r_y.at[i],
                                         ypart))
        for n in range(NZ)
    ]

    def shares(pair):
        for n in pair:
            wy_snd[n] = grad_share(n, 1 - yh)
            for cp in y_copies[n]:
                cp.start()
        for n in pair:
            w_own[n] = grad_share(n, yh)

    cand_a = mine[0:1, 0:1]
    cand_b = theirs[0:1, 0:1]

    def term(n, r):
        y_copies[n][r].wait_recv()
        a, b = w_own[n, r].astype(F32), wy_rcv[n, r].astype(F32)
        return [
            jnp.where(cand_a == c, a, 0.0) + jnp.where(cand_b == c, b, 0.0) for c in (0, 1)
        ]

    def hops(snd, rcv, ssem, rsem, to):
        return [
            pieces(t, lambda t, r, i: remote(snd.at[t, r], rcv.at[t, r], ssem.at[i], rsem.at[i], to))
            for t in range(4)
        ]

    downs = hops(rm_snd, rm_rcv, s_m, r_m, zdn)
    ups = hops(rp_snd, rp_rcv, s_q, r_q, zup)

    def ring(ring_hops, snd, rcv, t, n, first):
        for r in range(NR):
            if t == 0 and r != first:
                continue
            values = term(n, r)
            more = t > 1 or (t == 1 and r == first)
            if more:
                ring_hops[t - 1][r].wait_recv()
            for c in (0, 1):
                value = values[c]
                if more:
                    value = value + rcv[t - 1, r, c].astype(F32)
                snd[t, r, c] = value.astype(BF16)
            ring_hops[t][r].start()

    def down(t):
        ring(downs, rm_snd, rm_rcv, t, 4 + t, 0)

    def up(t):
        ring(ups, rp_snd, rp_rcv, t, 4 - t, 1)

    def d_hidden(c):
        got = None
        for n in CHUNKS[c]:
            for yd in (0, 1):
                at = cols(owner[n] * 2 + yd)
                part = lax.dot_general(rows_of(n, yd), wdv[:, at], NT, preferred_element_type=F32)
                got = part if got is None else got + part
        if c == 0:
            dhv[...] = got
        else:
            dhv[...] += got

    grads[0].arrive()
    shares(CHUNKS[0])
    d_hidden(0)
    grads[1].arrive()
    shares(CHUNKS[1])
    down(0)
    up(0)
    d_hidden(1)
    grads[2].arrive()
    shares(CHUNKS[2])
    up(1)
    down(1)
    d_hidden(2)
    grads[3].arrive()
    shares(CHUNKS[3])
    d_hidden(3)
    d_hid = dhv[...]
    dgv[...] = (d_hid * pre_up * sig * (1.0 + pre_gate * (1.0 - sig))).astype(BF16)
    duv[...] = (d_hid * act).astype(BF16)
    up(2)
    down(2)

    def partial(start):
        at = pl.ds(pl.multiple_of(start, CH), CH)
        got = jnp.dot(dgv[...], wgv[:, at], preferred_element_type=F32)
        return got + jnp.dot(duv[...], wuv[:, at], preferred_element_type=F32)

    p_copies = [
        remote(p_snd.at[c], p_rcv.at[c], s_p.at[c], r_p.at[c], sib) for c in range(NC)
    ]
    for c in range(NC):
        got = partial((1 - k) * HALF + c * CH)
        p_snd[c] = got.astype(BF16).reshape(CHIPS, PAIR, CH)
        p_copies[c].start()
    for c in range(NC):
        p_own[c] = partial(k * HALF + c * CH).reshape(CHIPS, PAIR, CH)

    r_copies = []

    def send_back(c):
        def both_cores(chip):
            return (p_own[c, chip] + p_rcv[c, chip].astype(F32)).astype(BF16)

        p_copies[c].wait()
        sent = []
        for i in range(3):
            for j, (base, dst) in enumerate((((1 - yl) * NX, relr), (yl * NX, fin))):
                at = 2 * i + j
                r_snd[c, at] = both_cores(base + x_of[i])
                cp = remote(r_snd.at[c, at], dst.at[c, x],
                            s_r.at[6 * c + at], r_r.at[6 * c + at], along[i])
                cp.start()
                sent.append(cp)
        relr[c, x] = both_cores(q_far)
        fin[c, x] = both_cores(q)
        r_copies.append(sent)

    up(3)
    down(3)
    for c in range(NC):
        send_back(c)

    d_copies = []

    def use(n, zo, r):
        at, rows = cols(zo * 2 + yh), slice(r * PIECE, (r + 1) * PIECE)
        first, second = dall[zo, r, 0].astype(F32), dall[zo, r, 1].astype(F32)
        dy[n, r] = jnp.where(cand_b == 0, first, second).astype(BF16)
        i = NR * n + r
        cp = remote(dy.at[n, r], sd_out.at[0, rows, at], s_d.at[i], r_d.at[i], ypart)
        cp.start()
        d_copies.append(cp)
        sd_out[0, rows, at] = jnp.where(cand_a == 0, first, second).astype(BF16)

    below = [lax.rem(z + NZ - t, NZ) for t in range(5)]
    above = [lax.rem(z + t, NZ) for t in range(5)]

    def passes(zo, ssem, rsem, t, to):
        return pieces(t, lambda t, r, i: remote(dall.at[zo, r], dall.at[zo, r], ssem.at[i],
                                                rsem.at[i], to))

    a_up = [passes(below[t], s_ap, r_ap, t, zup) for t in range(4)]
    a_dn = [passes(above[t], s_am, r_am, t, zdn) for t in range(4)]

    for r in range(NR):
        rows = slice(r * PIECE, (r + 1) * PIECE)
        grads_r = term(0, r)
        ups[3][r].wait_recv()
        downs[3][r].wait_recv()
        for c in (0, 1):
            grad = grads_r[c] + rp_rcv[3, r, c].astype(F32) + rm_rcv[3, r, c].astype(F32)
            first = beta_one * m1v[c, rows] + (1.0 - beta_one) * grad
            second = beta_two * m2v[c, rows] + (1.0 - beta_two) * grad * grad
            nf_out[c, rows] = first
            ns_out[c, rows] = second
            step = first / first_fix / (jnp.sqrt(second / second_fix) + adam_eps)
            dall[z, r, c] = step.astype(BF16)
        a_up[0][r].start()
        a_dn[0][r].start()
        use(0, z, r)

    far_copies = []

    def relay_back(c):
        for cp in r_copies[c]:
            cp.wait_recv()
        for p in (0, 1):
            got = relr[c, 2 * p].astype(F32) + relr[c, 2 * p + 1].astype(F32)
            rel_s[c, p] = got.astype(BF16)
            at = 2 * c + p
            cp = remote(rel_s.at[c, p], rback.at[c, row_slots + p], s_ry.at[at], r_ry.at[at], far)
            cp.start()
            far_copies.append(cp)
        for p in (0, 1):
            got = fin[c, 2 * p].astype(F32) + fin[c, 2 * p + 1].astype(F32)
            rback[c, row_slots + p] = got.astype(BF16)

    tg_copies = []

    def combine(c):
        for cp in far_copies[2 * c : 2 * c + 2]:
            cp.wait_recv()
        rows = rback[c].reshape(SLOTS * PAIR, CH)
        for kk in (0, 1):
            got = jnp.dot(sel_t[kk], rows, preferred_element_type=F32)
            tgv[c, kk] = got.astype(BF16)
        at = pl.ds(pl.multiple_of(k * HALF + c * CH, CH), CH)
        cp = remote(tgv.at[c, 1 - k], tg_out.at[:, at], s_tg.at[c], r_tg.at[c], sib)
        cp.start()
        tg_copies.append(cp)
        tg_out[:, at] = tgv[c, k]

    for t in range(4):
        for r in range(NR):
            if t < 3 or r == 0:
                a_up[t][r].wait_recv()
                if t < 2 or (t == 2 and r == 0):
                    a_up[t + 1][r].start()
                use(1 + t, below[t + 1], r)
            if t < 3 or r == 1:
                a_dn[t][r].wait_recv()
                if t < 2 or (t == 2 and r == 1):
                    a_dn[t + 1][r].start()
                use(5 + t if t < 3 else 4, above[t + 1], r)
        if t == 0:
            relay_back(0)
            relay_back(1)
        if t == 1:
            relay_back(2)
            relay_back(3)
            combine(0)
        if t == 2:
            combine(1)
            combine(2)
    combine(3)

    for cp in tg_copies + d_copies:
        cp.wait()
    for r in [toks] + grads:
        r.end()
    for cp in far_copies:
        cp.wait_send()
    for sent in r_copies + y_copies:
        for cp in sent:
            cp.wait_send()
    for t in range(4):
        for c in (0, 1):
            if t > 0 or c == 0:
                downs[t][c].wait_send()
            if t > 0 or c == 1:
                ups[t][c].wait_send()
            if t < 3 or c == 0:
                a_up[t][c].wait_send()
            if t < 3 or c == 1:
                a_dn[t][c].wait_send()


def step(tokens, expert_ids, gate_probs, placement, gate_weight, up_weight, down_weight,
         out_grad, moment_first, moment_second):
    def vm(*shape, dtype=BF16):
        return pltpu.VMEM(shape, dtype)

    dma = lambda n: pltpu.SemaphoreType.DMA((n,))
    anywhere = pl.BlockSpec(memory_space=pl.ANY)
    outs = pl.pallas_call(
        body,
        out_shape=(
            vm(TOK, D), vm(1, HU, D), vm(2, HU, SHARE, dtype=F32), vm(2, HU, SHARE, dtype=F32),
        ),
        in_specs=[anywhere] * 3 + [pl.BlockSpec(memory_space=pltpu.SMEM)] + [anywhere] * 6,
        out_specs=(pl.BlockSpec(memory_space=pltpu.VMEM),) * 4,
        scratch_shapes=[
            vm(2, TOK, HALF), vm(2, NZ, TOK, SHARE),
            vm(2, 8, TOK, dtype=jnp.int32), vm(2, 8, TOK, dtype=F32),
            vm(2, TOK, SLOTS * PAIR),
            vm(SLOTS, PAIR, HALF), vm(NC, SLOTS, PAIR, CH),
            vm(2, PAIR, HALF), vm(NC, 2, PAIR, CH),
            vm(2, CHIPS, PAIR, HALF), vm(2, NC, CHIPS, PAIR, CH),
            vm(HU, D), vm(HU, D), vm(HU, D),
            vm(2, HU, SHARE, dtype=F32), vm(2, HU, SHARE, dtype=F32),
            vm(HU, ROWS), vm(ROWS, HU, dtype=F32), vm(ROWS, HU), vm(ROWS, HU),
            vm(NC, CHIPS, PAIR, CH), vm(NC, CHIPS, PAIR, CH),
            vm(NC, CHIPS, PAIR, CH, dtype=F32),
            vm(NC, 6, PAIR, CH), vm(NC, NX, PAIR, CH), vm(NC, NX, PAIR, CH),
            vm(NC, 2, PAIR, CH), vm(NC, SLOTS, PAIR, CH), vm(NC, 2, TOK, CH),
            vm(8, 128, dtype=jnp.int32), vm(8, 128, dtype=jnp.int32),
            vm(NZ, NR, PIECE, SHARE), vm(NZ, NR, PIECE, SHARE), vm(NZ, NR, PIECE, SHARE),
            vm(4, NR, 2, PIECE, SHARE), vm(4, NR, 2, PIECE, SHARE),
            vm(4, NR, 2, PIECE, SHARE), vm(4, NR, 2, PIECE, SHARE),
            vm(NZ, NR, 2, PIECE, SHARE), vm(NZ, NR, PIECE, SHARE),
            dma(16), dma(11), dma(11),
            dma(2), dma(2), dma(2), dma(6), dma(6), dma(8), dma(8),
            dma(2 * NC), dma(2 * NC), dma(2 * NC), dma(6 * NC), dma(6 * NC), dma(8 * NC),
            dma(8 * NC),
            dma(NC), dma(NC), dma(6 * NC), dma(6 * NC), dma(2 * NC), dma(2 * NC), dma(NC), dma(NC),
            dma(1), dma(1), dma(16), dma(16), dma(8), dma(8), dma(8), dma(8),
            dma(8), dma(8), dma(8), dma(8), dma(16), dma(16),
        ],
        compiler_params=pltpu.CompilerParams(
            collective_id=0, has_side_effects=True, vmem_limit_bytes=60 * 2**20
        ),
    )(tokens, expert_ids.T, gate_probs.T, placement, jnp.swapaxes(gate_weight, 1, 2),
      jnp.swapaxes(up_weight, 1, 2), down_weight, out_grad, moment_first, moment_second)
    return outs


def solution(mesh):
    return jax.shard_map(
        step,
        mesh=mesh,
        in_specs=(
            P(("grp", "ep"), None),
            P(("grp", "ep"), None),
            P(("grp", "ep"), None),
            P("grp", None),
            P("grp", None, "ep"),
            P("grp", None, "ep"),
            P("grp", "ep", None),
            P(("grp", "ep"), None),
            P(None, "ep", "grp"),
            P(None, "ep", "grp"),
        ),
        out_specs=(
            P(("grp", "ep"), None),
            P("grp", "ep", None),
            P(None, "ep", "grp"),
            P(None, "ep", "grp"),
        ),
        check_vma=False,
    )
```

```python
import math

import jax
import jax.numpy as jnp
from jax import lax
from jax.experimental import pallas as pl
from jax.experimental.pallas import tpu as pltpu
from jax.sharding import PartitionSpec as P

MESH = pl.DeviceIdType.MESH
F32 = jnp.float32
BF16 = jnp.bfloat16

D = 4096
HALF = 2048
TOK = 192
HU = 192
CAP = 24
PAIR = 2 * CAP
SLOTS = 4
CHIPS = 8
NX = 4
NZ = 8
SHARE = 256
ROWS = CHIPS * PAIR
CH = 512

beta_one = 0.9
beta_two = 0.999
adam_eps = 1e-08
first_fix = 1.0 - math.exp(1000.0 * math.log(0.9))
second_fix = 1.0 - math.exp(1000.0 * math.log(0.999))

XD = (2, 1, 3)
NC = 4
NTC = 2
TCH = HALF // NTC
NR = 2
PIECE = HU // NR
CHUNKS = ((4, 0), (3, 5), (2, 6), (1, 7))
NT = (((1,), (1,)), ((), ()))


def body(
    tok, ids, prb, plc, wg, wu, wd, og, m1, m2,
    tg_out, sd_out, nf_out, ns_out,
    tokH, grdH, idsH, prbH, sel_t, snd_t, snd_g, rel_t, rel_g, xt, xg,
    wgv, wuv, wdv, m1v, m2v, hid_t, dhv, dgv, duv,
    p_snd, p_rcv, p_own, r_snd, fin, relr, rel_s, rback, tgv,
    mine, theirs, wy_snd, wy_rcv, w_own,
    rm_snd, rm_rcv, rp_snd, rp_rcv, dall, dy,
    lsem, s_in, r_in,
    tl, tys, tyr, txs, txr, tfs, tfr, gl, gys, gyr, gxs, gxr, gfs, gfr,
    s_p, r_p, s_r, r_r, s_ry, r_ry, s_tg, r_tg,
    s_c, r_c, s_y, r_y, s_m, r_m, s_q, r_q, s_am, r_am, s_ap, r_ap, s_d, r_d,
):
    g = lax.axis_index("grp")
    e = lax.axis_index("ep")
    z, yh = g // 2, lax.rem(g, 2)
    q, k = e // 2, lax.rem(e, 2)
    yl, x = q // NX, lax.rem(q, NX)
    slot = q // 2
    row_slots, far_slots = yl * 2, (1 - yl) * 2
    side = x // 2
    q_far = (1 - yl) * NX + x
    sib = {"grp": g, "ep": q * 2 + 1 - k}
    far = {"grp": g, "ep": q_far * 2 + k}
    ypart = {"grp": z * 2 + 1 - yh, "ep": e}
    zup = {"grp": lax.rem(z + 1, NZ) * 2 + yh, "ep": e}
    zdn = {"grp": lax.rem(z + NZ - 1, NZ) * 2 + yh, "ep": e}
    x_of = [lax.rem(x + d, NX) for d in XD]
    x_from = [lax.rem(x - d + NX, NX) for d in XD]
    along = [{"grp": g, "ep": (yl * NX + xd) * 2 + k} for xd in x_of]

    def remote(src, dst, ssem, rsem, to):
        return pltpu.make_async_remote_copy(
            src_ref=src, dst_ref=dst, send_sem=ssem, recv_sem=rsem, device_id=to,
            device_id_type=MESH,
        )

    def cols(i):
        return pl.ds(pl.multiple_of(i * SHARE, SHARE), SHARE)

    mine_cols = pl.ds(pl.multiple_of(k * HALF, HALF), HALF)

    def tok_cols(core, c):
        return pl.ds(pl.multiple_of(core * HALF + c * TCH, TCH), TCH)

    local = [
        pltpu.make_async_copy(ids, idsH.at[k], lsem.at[0]),
        pltpu.make_async_copy(prb, prbH.at[k], lsem.at[1]),
    ] + [
        pltpu.make_async_copy(tok.at[:, tok_cols(k, c)], tokH.at[k, c], lsem.at[16 + c])
        for c in range(NTC)
    ]
    local_g = [
        pltpu.make_async_copy(og.at[:, cols(2 * i + k)], grdH.at[k, i], lsem.at[8 + i])
        for i in range(NZ)
    ]
    later = [
        pltpu.make_async_copy(wg.at[0], wgv, lsem.at[3]),
        pltpu.make_async_copy(wu.at[0], wuv, lsem.at[4]),
        pltpu.make_async_copy(wd.at[0], wdv, lsem.at[5]),
        pltpu.make_async_copy(m1, m1v, lsem.at[6]),
        pltpu.make_async_copy(m2, m2v, lsem.at[7]),
    ]
    for cp in local + local_g:
        cp.start()
    mine[...] = jnp.zeros((8, 128), jnp.int32) + plc[0, slot]

    barrier = pltpu.get_barrier_semaphore()
    greet = [sib, far, ypart, zup, zdn] + along
    for to in greet:
        pl.semaphore_signal(barrier, inc=1, device_id=to, device_id_type=MESH)
    pl.semaphore_wait(barrier, len(greet))

    swap = [
        remote(ids, idsH.at[k], s_in.at[0], r_in.at[0], sib),
        remote(prb, prbH.at[k], s_in.at[1], r_in.at[1], sib),
    ] + [
        remote(tok.at[:, tok_cols(1 - k, c)], tokH.at[k, c], s_in.at[11 + c], r_in.at[11 + c], sib)
        for c in range(NTC)
    ]
    swap_g = [
        remote(og.at[:, cols(2 * i + 1 - k)], grdH.at[k, i], s_in.at[3 + i], r_in.at[3 + i], sib)
        for i in range(NZ)
    ]
    for cp in swap + swap_g:
        cp.start()
    cand_copy = remote(mine, theirs, s_c.at[0], r_c.at[0], ypart)
    cand_copy.start()
    for cp in later:
        cp.start()

    for i in (0, 1):
        local[i].wait()
        swap[i].wait()
    row = lax.broadcasted_iota(jnp.int32, (TOK, TOK), 0)
    col = lax.broadcasted_iota(jnp.int32, (TOK, TOK), 1)
    before = jnp.where(row < col, 1.0, 0.0).astype(BF16)
    line = lax.broadcasted_iota(jnp.int32, (8, TOK), 0)
    r48 = lax.broadcasted_iota(jnp.int32, (PAIR, TOK), 0)
    place = jnp.where(r48 >= CAP, r48 - CAP, r48).astype(F32)
    pick_all = []
    scale_all = jnp.zeros((SLOTS * PAIR, 1), F32)
    for kk in (0, 1):
        id_rows, prob_rows = idsH[kk], prbH[kk]
        hits = jnp.zeros((8, TOK), F32)
        coefs = []
        for s in range(SLOTS):
            match = id_rows == plc[0, s] * SLOTS + s
            hit = jnp.max(jnp.where(match, 1.0, 0.0), axis=0, keepdims=True)
            coefs.append(jnp.sum(jnp.where(match, prob_rows, 0.0), axis=0, keepdims=True))
            hits = jnp.where(line == s, hit, hits)
        rank = jnp.dot(hits.astype(BF16), before, preferred_element_type=F32)
        own_rows = (r48 >= CAP) == (kk == 1)
        picks, scales = [], []
        for s in range(SLOTS):
            ok = own_rows & (hits[s : s + 1] > 0.5) & (rank[s : s + 1] == place)
            pick = jnp.where(ok, 1.0, 0.0)
            picks.append(pick)
            scales.append(jnp.sum(pick * coefs[s], axis=1, keepdims=True))
        pick = jnp.concatenate(picks, axis=0)
        scale_all += jnp.concatenate(scales, axis=0)
        sel_t[kk] = jnp.transpose(pick).astype(BF16)
        pick_all.append(pick.astype(BF16))

    def select(rows_a, rows_b):
        got = jnp.dot(pick_all[0], rows_a, preferred_element_type=F32)
        return got + jnp.dot(pick_all[1], rows_b, preferred_element_type=F32)

    class Route:
        def __init__(self, block, land, relay, sems, nth):
            ls, ys, yr, xs, xr, fs, fr = sems
            self.own = pltpu.make_async_copy(
                block(row_slots + side), land(q), ls.at[2 * nth]
            )
            self.own_far = pltpu.make_async_copy(
                relay(side), land(q_far), ls.at[2 * nth + 1]
            )
            self.y = [
                remote(block(far_slots + p), relay(p), ys.at[2 * nth + p], yr.at[2 * nth + p], far)
                for p in (0, 1)
            ]
            self.x_near, self.x_far = [], []
            for i in range(3):
                there, at = x_of[i] // 2, 6 * nth + i
                self.x_near.append(remote(block(row_slots + there), land(q),
                                          xs.at[at], xr.at[at], along[i]))
                self.x_far.append(remote(relay(there), land(q_far),
                                         xs.at[at + 3], xr.at[at + 3], along[i]))
            at = 8 * nth
            self.f_own = remote(block(row_slots + side), land(q), fs.at[at], fr.at[at], sib)
            self.f_far = remote(relay(side), land(q_far), fs.at[at + 1], fr.at[at + 1], sib)
            self.f_near_x, self.f_far_x = [], []
            for i in range(3):
                for kept, base, off in (
                    (self.f_near_x, yl * NX, 2), (self.f_far_x, (1 - yl) * NX, 5)
                ):
                    ref = land(base + x_from[i])
                    kept.append(remote(ref, ref, fs.at[at + off + i], fr.at[at + off + i], sib))

        def start_y(self):
            for cp in self.y:
                cp.start()

        def start_near(self):
            for cp in self.x_near:
                cp.start()
            self.own.start()
            self.f_own.start()

        def start_far(self):
            for cp in self.y:
                cp.wait_recv()
            for cp in self.x_far:
                cp.start()
            self.own_far.start()
            self.f_far.start()

        def arrive(self):
            for i in (1, 2, 0):
                self.x_near[i].wait_recv()
                self.f_near_x[i].start()
            for i in (1, 2, 0):
                self.x_far[i].wait_recv()
                self.f_far_x[i].start()
            for cp in [self.f_own, self.f_far] + self.f_near_x + self.f_far_x:
                cp.wait()
            self.own.wait()
            self.own_far.wait()

        def end(self):
            for cp in self.y + self.x_near + self.x_far:
                cp.wait_send()

    def tok_route(n):
        return Route(
            lambda s: snd_t.at[n, s], lambda chip: xt.at[k, n, chip], lambda p: rel_t.at[n, p],
            (tl, tys, tyr, txs, txr, tfs, tfr), n,
        )

    toks = [tok_route(n) for n in range(NTC)]
    owner = [lax.rem(z + n, NZ) for n in range(NZ)]

    def grad_route(n):
        return Route(
            lambda s: snd_g.at[n, s], lambda chip: xg.at[k, n, chip], lambda p: rel_g.at[n, p],
            (gl, gys, gyr, gxs, gxr, gfs, gfr), n,
        )

    grads = [grad_route(n) for n in range(NC)]

    for n in range(NTC):
        local[2 + n].wait()
        swap[2 + n].wait()
        for c in range(0, TCH, CH):
            at = slice(c, c + CH)
            got = select(tokH[0, n, :, at], tokH[1, n, :, at])
            snd_t[n, :, :, at] = got.astype(BF16).reshape(SLOTS, PAIR, CH)
        toks[n].start_y()
        toks[n].start_near()
    for cp in local_g + swap_g:
        cp.wait()
    for c, pair in enumerate(CHUNKS):
        for j, n in enumerate(pair):
            got = select(grdH[0, owner[n]], grdH[1, owner[n]]) * scale_all
            at = slice(j * SHARE, (j + 1) * SHARE)
            snd_g[c, :, :, at] = got.astype(BF16).reshape(SLOTS, PAIR, SHARE)
    for r in grads:
        r.start_y()
    grads[0].start_near()
    for r in toks:
        r.start_far()
    grads[0].start_far()
    for n in range(1, NC):
        grads[n].start_near()
        grads[n].start_far()
    for cp in later:
        cp.wait()
    cand_copy.wait()

    for r in toks:
        r.arrive()
    pre_gate = jnp.zeros((ROWS, HU), F32)
    pre_up = jnp.zeros((ROWS, HU), F32)
    for c in range(0, D, CH):
        at = c % TCH
        rows = xt[c // HALF, c % HALF // TCH, :, :, at : at + CH].reshape(ROWS, CH)
        pre_gate += lax.dot_general(rows, wgv[:, c : c + CH], NT, preferred_element_type=F32)
        pre_up += lax.dot_general(rows, wuv[:, c : c + CH], NT, preferred_element_type=F32)
    sig = jax.nn.sigmoid(pre_gate)
    act = pre_gate * sig
    hid_t[...] = jnp.transpose(act * pre_up).astype(BF16)

    def rows_of(n, yd):
        [(c, j)] = [(c, pair.index(n)) for c, pair in enumerate(CHUNKS) if n in pair]
        return xg[yd, c, :, :, j * SHARE : (j + 1) * SHARE].reshape(ROWS, SHARE)

    def grad_share(n, yd):
        got = jnp.dot(hid_t[...], rows_of(n, yd), preferred_element_type=F32)
        return got.astype(BF16).reshape(NR, PIECE, SHARE)

    def pieces(n, make):
        return [make(n, r, NR * n + r) for r in range(NR)]

    y_copies = [
        pieces(n, lambda n, r, i: remote(wy_snd.at[n, r], wy_rcv.at[n, r], s_y.at[i], r_y.at[i],
                                         ypart))
        for n in range(NZ)
    ]

    def shares(pair):
        for n in pair:
            wy_snd[n] = grad_share(n, 1 - yh)
            for cp in y_copies[n]:
                cp.start()
        for n in pair:
            w_own[n] = grad_share(n, yh)

    cand_a = mine[0:1, 0:1]
    cand_b = theirs[0:1, 0:1]

    def term(n, r):
        y_copies[n][r].wait_recv()
        a, b = w_own[n, r].astype(F32), wy_rcv[n, r].astype(F32)
        return [
            jnp.where(cand_a == c, a, 0.0) + jnp.where(cand_b == c, b, 0.0) for c in (0, 1)
        ]

    def hops(snd, rcv, ssem, rsem, to):
        return [
            pieces(t, lambda t, r, i: remote(snd.at[t, r], rcv.at[t, r], ssem.at[i], rsem.at[i], to))
            for t in range(4)
        ]

    downs = hops(rm_snd, rm_rcv, s_m, r_m, zdn)
    ups = hops(rp_snd, rp_rcv, s_q, r_q, zup)

    def ring(ring_hops, snd, rcv, t, n, first):
        for r in range(NR):
            if t == 0 and (r < NR // 2) != first:
                continue
            values = term(n, r)
            more = t > 1 or (t == 1 and (r < NR // 2) == first)
            if more:
                ring_hops[t - 1][r].wait_recv()
            for c in (0, 1):
                value = values[c]
                if more:
                    value = value + rcv[t - 1, r, c].astype(F32)
                snd[t, r, c] = value.astype(BF16)
            ring_hops[t][r].start()

    def down(t):
        ring(downs, rm_snd, rm_rcv, t, 4 + t, True)

    def up(t):
        ring(ups, rp_snd, rp_rcv, t, 4 - t, False)

    def d_hidden(c):
        got = None
        for n in CHUNKS[c]:
            for yd in (0, 1):
                at = cols(owner[n] * 2 + yd)
                part = lax.dot_general(rows_of(n, yd), wdv[:, at], NT, preferred_element_type=F32)
                got = part if got is None else got + part
        if c == 0:
            dhv[...] = got
        else:
            dhv[...] += got

    grads[0].arrive()
    shares(CHUNKS[0])
    d_hidden(0)
    grads[1].arrive()
    shares(CHUNKS[1])
    down(0)
    up(0)
    d_hidden(1)
    grads[2].arrive()
    shares(CHUNKS[2])
    up(1)
    down(1)
    d_hidden(2)
    grads[3].arrive()
    shares(CHUNKS[3])
    d_hidden(3)
    d_hid = dhv[...]
    dgv[...] = (d_hid * pre_up * sig * (1.0 + pre_gate * (1.0 - sig))).astype(BF16)
    duv[...] = (d_hid * act).astype(BF16)
    up(2)
    down(2)

    def partial(start):
        at = pl.ds(pl.multiple_of(start, CH), CH)
        got = jnp.dot(dgv[...], wgv[:, at], preferred_element_type=F32)
        return got + jnp.dot(duv[...], wuv[:, at], preferred_element_type=F32)

    p_copies = [
        remote(p_snd.at[c], p_rcv.at[c], s_p.at[c], r_p.at[c], sib) for c in range(NC)
    ]
    for c in range(NC):
        got = partial((1 - k) * HALF + c * CH)
        p_snd[c] = got.astype(BF16).reshape(CHIPS, PAIR, CH)
        p_copies[c].start()
    for c in range(NC):
        p_own[c] = partial(k * HALF + c * CH).reshape(CHIPS, PAIR, CH)

    r_copies = []

    def send_back(c):
        def both_cores(chip):
            return (p_own[c, chip] + p_rcv[c, chip].astype(F32)).astype(BF16)

        p_copies[c].wait()
        sent = []
        for i in range(3):
            for j, (base, dst) in enumerate((((1 - yl) * NX, relr), (yl * NX, fin))):
                at = 2 * i + j
                r_snd[c, at] = both_cores(base + x_of[i])
                cp = remote(r_snd.at[c, at], dst.at[c, x],
                            s_r.at[6 * c + at], r_r.at[6 * c + at], along[i])
                cp.start()
                sent.append(cp)
        relr[c, x] = both_cores(q_far)
        fin[c, x] = both_cores(q)
        r_copies.append(sent)

    up(3)
    down(3)
    for c in range(NC):
        send_back(c)

    d_copies = []

    def use(n, zo, r):
        at, rows = cols(zo * 2 + yh), slice(r * PIECE, (r + 1) * PIECE)
        first, second = dall[zo, r, 0].astype(F32), dall[zo, r, 1].astype(F32)
        dy[n, r] = jnp.where(cand_b == 0, first, second).astype(BF16)
        i = NR * n + r
        cp = remote(dy.at[n, r], sd_out.at[0, rows, at], s_d.at[i], r_d.at[i], ypart)
        cp.start()
        d_copies.append(cp)
        sd_out[0, rows, at] = jnp.where(cand_a == 0, first, second).astype(BF16)

    below = [lax.rem(z + NZ - t, NZ) for t in range(5)]
    above = [lax.rem(z + t, NZ) for t in range(5)]

    def passes(zo, ssem, rsem, t, to):
        return pieces(t, lambda t, r, i: remote(dall.at[zo, r], dall.at[zo, r], ssem.at[i],
                                                rsem.at[i], to))

    a_up = [passes(below[t], s_ap, r_ap, t, zup) for t in range(4)]
    a_dn = [passes(above[t], s_am, r_am, t, zdn) for t in range(4)]

    for r in range(NR):
        rows = slice(r * PIECE, (r + 1) * PIECE)
        grads_r = term(0, r)
        ups[3][r].wait_recv()
        downs[3][r].wait_recv()
        for c in (0, 1):
            grad = grads_r[c] + rp_rcv[3, r, c].astype(F32) + rm_rcv[3, r, c].astype(F32)
            first = beta_one * m1v[c, rows] + (1.0 - beta_one) * grad
            second = beta_two * m2v[c, rows] + (1.0 - beta_two) * grad * grad
            nf_out[c, rows] = first
            ns_out[c, rows] = second
            step = first / first_fix / (jnp.sqrt(second / second_fix) + adam_eps)
            dall[z, r, c] = step.astype(BF16)
        a_up[0][r].start()
        a_dn[0][r].start()
        use(0, z, r)

    far_copies = []

    def relay_back(c):
        for cp in r_copies[c]:
            cp.wait_recv()
        for p in (0, 1):
            got = relr[c, 2 * p].astype(F32) + relr[c, 2 * p + 1].astype(F32)
            rel_s[c, p] = got.astype(BF16)
            at = 2 * c + p
            cp = remote(rel_s.at[c, p], rback.at[c, row_slots + p], s_ry.at[at], r_ry.at[at], far)
            cp.start()
            far_copies.append(cp)
        for p in (0, 1):
            got = fin[c, 2 * p].astype(F32) + fin[c, 2 * p + 1].astype(F32)
            rback[c, row_slots + p] = got.astype(BF16)

    tg_copies = []

    def combine(c):
        for cp in far_copies[2 * c : 2 * c + 2]:
            cp.wait_recv()
        rows = rback[c].reshape(SLOTS * PAIR, CH)
        for kk in (0, 1):
            got = jnp.dot(sel_t[kk], rows, preferred_element_type=F32)
            tgv[c, kk] = got.astype(BF16)
        at = pl.ds(pl.multiple_of(k * HALF + c * CH, CH), CH)
        cp = remote(tgv.at[c, 1 - k], tg_out.at[:, at], s_tg.at[c], r_tg.at[c], sib)
        cp.start()
        tg_copies.append(cp)
        tg_out[:, at] = tgv[c, k]

    for t in range(4):
        for r in range(NR):
            if t < 3 or r < NR // 2:
                a_up[t][r].wait_recv()
                if t < 2 or (t == 2 and r < NR // 2):
                    a_up[t + 1][r].start()
                use(1 + t, below[t + 1], r)
            if t < 3 or r >= NR // 2:
                a_dn[t][r].wait_recv()
                if t < 2 or (t == 2 and r >= NR // 2):
                    a_dn[t + 1][r].start()
                use(5 + t if t < 3 else 4, above[t + 1], r)
        if t == 0:
            relay_back(0)
            relay_back(1)
        if t == 1:
            relay_back(2)
            relay_back(3)
            combine(0)
        if t == 2:
            combine(1)
            combine(2)
    combine(3)

    for cp in tg_copies + d_copies:
        cp.wait()
    for r in toks + grads:
        r.end()
    for cp in far_copies:
        cp.wait_send()
    for sent in r_copies + y_copies:
        for cp in sent:
            cp.wait_send()
    for t in range(4):
        for r in range(NR):
            low = r < NR // 2
            if t > 0 or low:
                downs[t][r].wait_send()
            if t > 0 or not low:
                ups[t][r].wait_send()
            if t < 3 or low:
                a_up[t][r].wait_send()
            if t < 3 or not low:
                a_dn[t][r].wait_send()


def store(*refs):
    sems = refs[-1]
    copies = [pltpu.make_async_copy(refs[i], refs[4 + i], sems.at[i]) for i in range(4)]
    for cp in copies:
        cp.start()
    for cp in copies:
        cp.wait()


def step(tokens, expert_ids, gate_probs, placement, gate_weight, up_weight, down_weight,
         out_grad, moment_first, moment_second):
    def vm(*shape, dtype=BF16):
        return pltpu.VMEM(shape, dtype)

    dma = lambda n: pltpu.SemaphoreType.DMA((n,))
    anywhere = pl.BlockSpec(memory_space=pl.ANY)
    outs = pl.pallas_call(
        body,
        out_shape=(
            vm(TOK, D), vm(1, HU, D), vm(2, HU, SHARE, dtype=F32), vm(2, HU, SHARE, dtype=F32),
        ),
        in_specs=[anywhere] * 3 + [pl.BlockSpec(memory_space=pltpu.SMEM)] + [anywhere] * 6,
        out_specs=(pl.BlockSpec(memory_space=pltpu.VMEM),) * 4,
        scratch_shapes=[
            vm(2, NTC, TOK, TCH), vm(2, NZ, TOK, SHARE),
            vm(2, 8, TOK, dtype=jnp.int32), vm(2, 8, TOK, dtype=F32),
            vm(2, TOK, SLOTS * PAIR),
            vm(NTC, SLOTS, PAIR, TCH), vm(NC, SLOTS, PAIR, CH),
            vm(NTC, 2, PAIR, TCH), vm(NC, 2, PAIR, CH),
            vm(2, NTC, CHIPS, PAIR, TCH), vm(2, NC, CHIPS, PAIR, CH),
            vm(HU, D), vm(HU, D), vm(HU, D),
            vm(2, HU, SHARE, dtype=F32), vm(2, HU, SHARE, dtype=F32),
            vm(HU, ROWS), vm(ROWS, HU, dtype=F32), vm(ROWS, HU), vm(ROWS, HU),
            vm(NC, CHIPS, PAIR, CH), vm(NC, CHIPS, PAIR, CH),
            vm(NC, CHIPS, PAIR, CH, dtype=F32),
            vm(NC, 6, PAIR, CH), vm(NC, NX, PAIR, CH), vm(NC, NX, PAIR, CH),
            vm(NC, 2, PAIR, CH), vm(NC, SLOTS, PAIR, CH), vm(NC, 2, TOK, CH),
            vm(8, 128, dtype=jnp.int32), vm(8, 128, dtype=jnp.int32),
            vm(NZ, NR, PIECE, SHARE), vm(NZ, NR, PIECE, SHARE), vm(NZ, NR, PIECE, SHARE),
            vm(4, NR, 2, PIECE, SHARE), vm(4, NR, 2, PIECE, SHARE),
            vm(4, NR, 2, PIECE, SHARE), vm(4, NR, 2, PIECE, SHARE),
            vm(NZ, NR, 2, PIECE, SHARE), vm(NZ, NR, PIECE, SHARE),
            dma(16 + NTC), dma(11 + NTC), dma(11 + NTC),
            dma(2 * NTC), dma(2 * NTC), dma(2 * NTC), dma(6 * NTC), dma(6 * NTC), dma(8 * NTC),
            dma(8 * NTC),
            dma(2 * NC), dma(2 * NC), dma(2 * NC), dma(6 * NC), dma(6 * NC), dma(8 * NC),
            dma(8 * NC),
            dma(NC), dma(NC), dma(6 * NC), dma(6 * NC), dma(2 * NC), dma(2 * NC), dma(NC), dma(NC),
            dma(1), dma(1), dma(NZ * NR), dma(NZ * NR),
            dma(4 * NR), dma(4 * NR), dma(4 * NR), dma(4 * NR),
            dma(4 * NR), dma(4 * NR), dma(4 * NR), dma(4 * NR), dma(NZ * NR), dma(NZ * NR),
        ],
        compiler_params=pltpu.CompilerParams(
            collective_id=0, has_side_effects=True, vmem_limit_bytes=60 * 2**20
        ),
    )(tokens, expert_ids.T, gate_probs.T, placement, jnp.swapaxes(gate_weight, 1, 2),
      jnp.swapaxes(up_weight, 1, 2), down_weight, out_grad, moment_first, moment_second)
    return pl.pallas_call(
        store,
        out_shape=tuple(jax.ShapeDtypeStruct(o.shape, o.dtype) for o in outs),
        in_specs=[pl.BlockSpec(memory_space=pltpu.VMEM)] * 4,
        out_specs=(anywhere,) * 4,
        scratch_shapes=[dma(4)],
        compiler_params=pltpu.CompilerParams(vmem_limit_bytes=2**20),
    )(*[pltpu.with_memory_space_constraint(o, pltpu.VMEM) for o in outs])


def solution(mesh):
    return jax.shard_map(
        step,
        mesh=mesh,
        in_specs=(
            P(("grp", "ep"), None),
            P(("grp", "ep"), None),
            P(("grp", "ep"), None),
            P("grp", None),
            P("grp", None, "ep"),
            P("grp", None, "ep"),
            P("grp", "ep", None),
            P(("grp", "ep"), None),
            P(None, "ep", "grp"),
            P(None, "ep", "grp"),
        ),
        out_specs=(
            P(("grp", "ep"), None),
            P("grp", "ep", None),
            P(None, "ep", "grp"),
            P(None, "ep", "grp"),
        ),
        check_vma=False,
    )
```

```python
import math

import jax
import jax.numpy as jnp
from jax import lax
from jax.experimental import pallas as pl
from jax.experimental.pallas import tpu as pltpu
from jax.sharding import PartitionSpec as P

MESH = pl.DeviceIdType.MESH
F32 = jnp.float32
BF16 = jnp.bfloat16

D = 4096
HALF = 2048
TOK = 192
HU = 192
CAP = 24
PAIR = 2 * CAP
SLOTS = 4
CHIPS = 8
NX = 4
NZ = 8
SHARE = 256
ROWS = CHIPS * PAIR
CH = 512

beta_one = 0.9
beta_two = 0.999
adam_eps = 1e-08
first_fix = 1.0 - math.exp(1000.0 * math.log(0.9))
second_fix = 1.0 - math.exp(1000.0 * math.log(0.999))

XD = (2, 1, 3)
NC = 4
NTC = 2
TCH = HALF // NTC
NR = 2
PIECE = HU // NR
CHUNKS = ((4, 0), (3, 5), (2, 6), (1, 7))
NT = (((1,), (1,)), ((), ()))


def body(
    tok, ids, prb, plc, wg, wu, wd, og, m1, m2,
    tg_out, sd_out, nf_out, ns_out,
    tokH, grdH, idsH, prbH, sel_t, snd_t, snd_g, rel_t, rel_g, xt, xg,
    wgv, wuv, wdv, m1v, m2v, hid_t, dhv, dgv, duv,
    p_snd, p_rcv, p_own, r_snd, fin, relr, rel_s, rback, tgv,
    mine, theirs, wy_snd, wy_rcv, w_own,
    rm_snd, rm_rcv, rp_snd, rp_rcv, dall, dy,
    lsem, s_in, r_in,
    tl, tys, tyr, txs, txr, tfs, tfr, gl, gys, gyr, gxs, gxr, gfs, gfr,
    s_p, r_p, s_r, r_r, s_ry, r_ry, s_tg, r_tg,
    s_c, r_c, s_y, r_y, s_m, r_m, s_q, r_q, s_am, r_am, s_ap, r_ap, s_d, r_d,
):
    g = lax.axis_index("grp")
    e = lax.axis_index("ep")
    z, yh = g // 2, lax.rem(g, 2)
    q, k = e // 2, lax.rem(e, 2)
    yl, x = q // NX, lax.rem(q, NX)
    slot = q // 2
    row_slots, far_slots = yl * 2, (1 - yl) * 2
    side = x // 2
    q_far = (1 - yl) * NX + x
    sib = {"grp": g, "ep": q * 2 + 1 - k}
    far = {"grp": g, "ep": q_far * 2 + k}
    ypart = {"grp": z * 2 + 1 - yh, "ep": e}
    zup = {"grp": lax.rem(z + 1, NZ) * 2 + yh, "ep": e}
    zdn = {"grp": lax.rem(z + NZ - 1, NZ) * 2 + yh, "ep": e}
    x_of = [lax.rem(x + d, NX) for d in XD]
    x_from = [lax.rem(x - d + NX, NX) for d in XD]
    along = [{"grp": g, "ep": (yl * NX + xd) * 2 + k} for xd in x_of]

    def remote(src, dst, ssem, rsem, to):
        return pltpu.make_async_remote_copy(
            src_ref=src, dst_ref=dst, send_sem=ssem, recv_sem=rsem, device_id=to,
            device_id_type=MESH,
        )

    def cols(i):
        return pl.ds(pl.multiple_of(i * SHARE, SHARE), SHARE)

    mine_cols = pl.ds(pl.multiple_of(k * HALF, HALF), HALF)

    def tok_cols(core, c):
        return pl.ds(pl.multiple_of(core * HALF + c * TCH, TCH), TCH)

    local = [
        pltpu.make_async_copy(ids, idsH.at[k], lsem.at[0]),
        pltpu.make_async_copy(prb, prbH.at[k], lsem.at[1]),
    ] + [
        pltpu.make_async_copy(tok.at[:, tok_cols(k, c)], tokH.at[k, c], lsem.at[16 + c])
        for c in range(NTC)
    ]
    local_g = [
        pltpu.make_async_copy(og.at[:, cols(2 * i + k)], grdH.at[k, i], lsem.at[8 + i])
        for i in range(NZ)
    ]
    later = [
        pltpu.make_async_copy(wg.at[0], wgv, lsem.at[3]),
        pltpu.make_async_copy(wu.at[0], wuv, lsem.at[4]),
        pltpu.make_async_copy(wd.at[0], wdv, lsem.at[5]),
        pltpu.make_async_copy(m1, m1v, lsem.at[6]),
        pltpu.make_async_copy(m2, m2v, lsem.at[7]),
    ]
    for cp in local + local_g:
        cp.start()
    mine[...] = jnp.zeros((8, 128), jnp.int32) + plc[0, slot]

    barrier = pltpu.get_barrier_semaphore()
    greet = [sib, far, ypart, zup, zdn] + along
    for to in greet:
        pl.semaphore_signal(barrier, inc=1, device_id=to, device_id_type=MESH)
    pl.semaphore_wait(barrier, len(greet))

    swap = [
        remote(ids, idsH.at[k], s_in.at[0], r_in.at[0], sib),
        remote(prb, prbH.at[k], s_in.at[1], r_in.at[1], sib),
    ] + [
        remote(tok.at[:, tok_cols(1 - k, c)], tokH.at[k, c], s_in.at[11 + c], r_in.at[11 + c], sib)
        for c in range(NTC)
    ]
    swap_g = [
        remote(og.at[:, cols(2 * i + 1 - k)], grdH.at[k, i], s_in.at[3 + i], r_in.at[3 + i], sib)
        for i in range(NZ)
    ]
    for cp in swap + swap_g:
        cp.start()
    cand_copy = remote(mine, theirs, s_c.at[0], r_c.at[0], ypart)
    cand_copy.start()
    for cp in later:
        cp.start()

    for i in (0, 1):
        local[i].wait()
        swap[i].wait()
    row = lax.broadcasted_iota(jnp.int32, (TOK, TOK), 0)
    col = lax.broadcasted_iota(jnp.int32, (TOK, TOK), 1)
    before = jnp.where(row < col, 1.0, 0.0).astype(BF16)
    line = lax.broadcasted_iota(jnp.int32, (8, TOK), 0)
    r48 = lax.broadcasted_iota(jnp.int32, (PAIR, TOK), 0)
    place = jnp.where(r48 >= CAP, r48 - CAP, r48).astype(F32)
    pick_all = []
    scale_all = jnp.zeros((SLOTS * PAIR, 1), F32)
    for kk in (0, 1):
        id_rows, prob_rows = idsH[kk], prbH[kk]
        hits = jnp.zeros((8, TOK), F32)
        coefs = []
        for s in range(SLOTS):
            match = id_rows == plc[0, s] * SLOTS + s
            hit = jnp.max(jnp.where(match, 1.0, 0.0), axis=0, keepdims=True)
            coefs.append(jnp.sum(jnp.where(match, prob_rows, 0.0), axis=0, keepdims=True))
            hits = jnp.where(line == s, hit, hits)
        rank = jnp.dot(hits.astype(BF16), before, preferred_element_type=F32)
        own_rows = (r48 >= CAP) == (kk == 1)
        picks, scales = [], []
        for s in range(SLOTS):
            ok = own_rows & (hits[s : s + 1] > 0.5) & (rank[s : s + 1] == place)
            pick = jnp.where(ok, 1.0, 0.0)
            picks.append(pick)
            scales.append(jnp.sum(pick * coefs[s], axis=1, keepdims=True))
        pick = jnp.concatenate(picks, axis=0)
        scale_all += jnp.concatenate(scales, axis=0)
        sel_t[kk] = jnp.transpose(pick).astype(BF16)
        pick_all.append(pick.astype(BF16))

    def select(rows_a, rows_b):
        got = jnp.dot(pick_all[0], rows_a, preferred_element_type=F32)
        return got + jnp.dot(pick_all[1], rows_b, preferred_element_type=F32)

    class Route:
        def __init__(self, block, land, relay, sems, nth):
            ls, ys, yr, xs, xr, fs, fr = sems
            self.own = pltpu.make_async_copy(
                block(row_slots + side), land(q), ls.at[2 * nth]
            )
            self.own_far = pltpu.make_async_copy(
                relay(side), land(q_far), ls.at[2 * nth + 1]
            )
            self.y = [
                remote(block(far_slots + p), relay(p), ys.at[2 * nth + p], yr.at[2 * nth + p], far)
                for p in (0, 1)
            ]
            self.x_near, self.x_far = [], []
            for i in range(3):
                there, at = x_of[i] // 2, 6 * nth + i
                self.x_near.append(remote(block(row_slots + there), land(q),
                                          xs.at[at], xr.at[at], along[i]))
                self.x_far.append(remote(relay(there), land(q_far),
                                         xs.at[at + 3], xr.at[at + 3], along[i]))
            at = 8 * nth
            self.f_own = remote(block(row_slots + side), land(q), fs.at[at], fr.at[at], sib)
            self.f_far = remote(relay(side), land(q_far), fs.at[at + 1], fr.at[at + 1], sib)
            self.f_near_x, self.f_far_x = [], []
            for i in range(3):
                for kept, base, off in (
                    (self.f_near_x, yl * NX, 2), (self.f_far_x, (1 - yl) * NX, 5)
                ):
                    ref = land(base + x_from[i])
                    kept.append(remote(ref, ref, fs.at[at + off + i], fr.at[at + off + i], sib))

        def start_y(self):
            for cp in self.y:
                cp.start()

        def start_near(self):
            for cp in self.x_near:
                cp.start()
            self.own.start()
            self.f_own.start()

        def start_far(self):
            for cp in self.y:
                cp.wait_recv()
            for cp in self.x_far:
                cp.start()
            self.own_far.start()
            self.f_far.start()

        def arrive(self):
            for i in (1, 2, 0):
                self.x_near[i].wait_recv()
                self.f_near_x[i].start()
            for i in (1, 2, 0):
                self.x_far[i].wait_recv()
                self.f_far_x[i].start()
            for cp in [self.f_own, self.f_far] + self.f_near_x + self.f_far_x:
                cp.wait()
            self.own.wait()
            self.own_far.wait()

        def end(self):
            for cp in self.y + self.x_near + self.x_far:
                cp.wait_send()

    def tok_route(n):
        return Route(
            lambda s: snd_t.at[n, s], lambda chip: xt.at[k, n, chip], lambda p: rel_t.at[n, p],
            (tl, tys, tyr, txs, txr, tfs, tfr), n,
        )

    toks = [tok_route(n) for n in range(NTC)]
    owner = [lax.rem(z + n, NZ) for n in range(NZ)]

    def grad_route(n):
        return Route(
            lambda s: snd_g.at[n, s], lambda chip: xg.at[k, n, chip], lambda p: rel_g.at[n, p],
            (gl, gys, gyr, gxs, gxr, gfs, gfr), n,
        )

    grads = [grad_route(n) for n in range(NC)]

    for n in range(NTC):
        local[2 + n].wait()
        swap[2 + n].wait()
        for c in range(0, TCH, CH):
            at = slice(c, c + CH)
            got = select(tokH[0, n, :, at], tokH[1, n, :, at])
            snd_t[n, :, :, at] = got.astype(BF16).reshape(SLOTS, PAIR, CH)
        toks[n].start_y()
        toks[n].start_near()
    for cp in local_g + swap_g:
        cp.wait()
    for c, pair in enumerate(CHUNKS):
        for j, n in enumerate(pair):
            got = select(grdH[0, owner[n]], grdH[1, owner[n]]) * scale_all
            at = slice(j * SHARE, (j + 1) * SHARE)
            snd_g[c, :, :, at] = got.astype(BF16).reshape(SLOTS, PAIR, SHARE)
    for r in grads:
        r.start_y()
    grads[0].start_near()
    for r in toks:
        r.start_far()
    grads[0].start_far()
    for n in range(1, NC):
        grads[n].start_near()
        grads[n].start_far()
    for cp in later:
        cp.wait()
    cand_copy.wait()

    for r in toks:
        r.arrive()
    pre_gate = jnp.zeros((ROWS, HU), F32)
    pre_up = jnp.zeros((ROWS, HU), F32)
    for c in range(0, D, CH):
        at = c % TCH
        rows = xt[c // HALF, c % HALF // TCH, :, :, at : at + CH].reshape(ROWS, CH)
        pre_gate += lax.dot_general(rows, wgv[:, c : c + CH], NT, preferred_element_type=F32)
        pre_up += lax.dot_general(rows, wuv[:, c : c + CH], NT, preferred_element_type=F32)
    sig = jax.nn.sigmoid(pre_gate)
    act = pre_gate * sig
    hid_t[...] = jnp.transpose(act * pre_up).astype(BF16)

    def rows_of(n, yd):
        [(c, j)] = [(c, pair.index(n)) for c, pair in enumerate(CHUNKS) if n in pair]
        return xg[yd, c, :, :, j * SHARE : (j + 1) * SHARE].reshape(ROWS, SHARE)

    def grad_share(n, yd):
        got = jnp.dot(hid_t[...], rows_of(n, yd), preferred_element_type=F32)
        return got.astype(BF16).reshape(NR, PIECE, SHARE)

    def pieces(n, make):
        return [make(n, r, NR * n + r) for r in range(NR)]

    y_copies = [
        pieces(n, lambda n, r, i: remote(wy_snd.at[n, r], wy_rcv.at[n, r], s_y.at[i], r_y.at[i],
                                         ypart))
        for n in range(NZ)
    ]

    def shares(pair):
        for n in pair:
            wy_snd[n] = grad_share(n, 1 - yh)
            for cp in y_copies[n]:
                cp.start()
        for n in pair:
            w_own[n] = grad_share(n, yh)

    cand_a = mine[0:1, 0:1]
    cand_b = theirs[0:1, 0:1]

    def term(n, r):
        y_copies[n][r].wait_recv()
        a, b = w_own[n, r].astype(F32), wy_rcv[n, r].astype(F32)
        return [
            jnp.where(cand_a == c, a, 0.0) + jnp.where(cand_b == c, b, 0.0) for c in (0, 1)
        ]

    def hops(snd, rcv, ssem, rsem, to):
        return [
            pieces(t, lambda t, r, i: remote(snd.at[t, r], rcv.at[t, r], ssem.at[i], rsem.at[i], to))
            for t in range(4)
        ]

    downs = hops(rm_snd, rm_rcv, s_m, r_m, zdn)
    ups = hops(rp_snd, rp_rcv, s_q, r_q, zup)

    def ring(ring_hops, snd, rcv, t, n, first):
        for r in range(NR):
            if t == 0 and (r < NR // 2) != first:
                continue
            values = term(n, r)
            more = t > 1 or (t == 1 and (r < NR // 2) == first)
            if more:
                ring_hops[t - 1][r].wait_recv()
            for c in (0, 1):
                value = values[c]
                if more:
                    value = value + rcv[t - 1, r, c].astype(F32)
                snd[t, r, c] = value.astype(BF16)
            ring_hops[t][r].start()

    def down(t):
        ring(downs, rm_snd, rm_rcv, t, 4 + t, True)

    def up(t):
        ring(ups, rp_snd, rp_rcv, t, 4 - t, False)

    def d_hidden(c):
        got = None
        for n in CHUNKS[c]:
            for yd in (0, 1):
                at = cols(owner[n] * 2 + yd)
                part = lax.dot_general(rows_of(n, yd), wdv[:, at], NT, preferred_element_type=F32)
                got = part if got is None else got + part
        if c == 0:
            dhv[...] = got
        else:
            dhv[...] += got

    grads[0].arrive()
    shares(CHUNKS[0])
    d_hidden(0)
    grads[1].arrive()
    shares(CHUNKS[1])
    down(0)
    up(0)
    d_hidden(1)
    grads[2].arrive()
    shares(CHUNKS[2])
    up(1)
    down(1)
    d_hidden(2)
    grads[3].arrive()
    shares(CHUNKS[3])
    up(2)
    down(2)
    d_hidden(3)
    d_hid = dhv[...]
    dgv[...] = (d_hid * pre_up * sig * (1.0 + pre_gate * (1.0 - sig))).astype(BF16)
    duv[...] = (d_hid * act).astype(BF16)

    def partial(start):
        at = pl.ds(pl.multiple_of(start, CH), CH)
        got = jnp.dot(dgv[...], wgv[:, at], preferred_element_type=F32)
        return got + jnp.dot(duv[...], wuv[:, at], preferred_element_type=F32)

    p_copies = [
        remote(p_snd.at[c], p_rcv.at[c], s_p.at[c], r_p.at[c], sib) for c in range(NC)
    ]
    for c in range(NC):
        got = partial((1 - k) * HALF + c * CH)
        p_snd[c] = got.astype(BF16).reshape(CHIPS, PAIR, CH)
        p_copies[c].start()
    up(3)
    down(3)
    for c in range(NC):
        p_own[c] = partial(k * HALF + c * CH).reshape(CHIPS, PAIR, CH)

    r_copies = []

    def send_back(c):
        def both_cores(chip):
            return (p_own[c, chip] + p_rcv[c, chip].astype(F32)).astype(BF16)

        p_copies[c].wait()
        sent = []
        for i in range(3):
            for j, (base, dst) in enumerate((((1 - yl) * NX, relr), (yl * NX, fin))):
                at = 2 * i + j
                r_snd[c, at] = both_cores(base + x_of[i])
                cp = remote(r_snd.at[c, at], dst.at[c, x],
                            s_r.at[6 * c + at], r_r.at[6 * c + at], along[i])
                cp.start()
                sent.append(cp)
        relr[c, x] = both_cores(q_far)
        fin[c, x] = both_cores(q)
        r_copies.append(sent)

    for c in range(NC):
        send_back(c)

    d_copies = []

    def use(n, zo, r):
        at, rows = cols(zo * 2 + yh), slice(r * PIECE, (r + 1) * PIECE)
        first, second = dall[zo, r, 0].astype(F32), dall[zo, r, 1].astype(F32)
        dy[n, r] = jnp.where(cand_b == 0, first, second).astype(BF16)
        i = NR * n + r
        cp = remote(dy.at[n, r], sd_out.at[0, rows, at], s_d.at[i], r_d.at[i], ypart)
        cp.start()
        d_copies.append(cp)
        sd_out[0, rows, at] = jnp.where(cand_a == 0, first, second).astype(BF16)

    below = [lax.rem(z + NZ - t, NZ) for t in range(5)]
    above = [lax.rem(z + t, NZ) for t in range(5)]

    def passes(zo, ssem, rsem, t, to):
        return pieces(t, lambda t, r, i: remote(dall.at[zo, r], dall.at[zo, r], ssem.at[i],
                                                rsem.at[i], to))

    a_up = [passes(below[t], s_ap, r_ap, t, zup) for t in range(4)]
    a_dn = [passes(above[t], s_am, r_am, t, zdn) for t in range(4)]

    for r in range(NR):
        rows = slice(r * PIECE, (r + 1) * PIECE)
        grads_r = term(0, r)
        ups[3][r].wait_recv()
        downs[3][r].wait_recv()
        for c in (0, 1):
            grad = grads_r[c] + rp_rcv[3, r, c].astype(F32) + rm_rcv[3, r, c].astype(F32)
            first = beta_one * m1v[c, rows] + (1.0 - beta_one) * grad
            second = beta_two * m2v[c, rows] + (1.0 - beta_two) * grad * grad
            nf_out[c, rows] = first
            ns_out[c, rows] = second
            step = first / first_fix / (jnp.sqrt(second / second_fix) + adam_eps)
            dall[z, r, c] = step.astype(BF16)
        a_up[0][r].start()
        a_dn[0][r].start()
        use(0, z, r)

    far_copies = []

    def relay_back(c):
        for cp in r_copies[c]:
            cp.wait_recv()
        for p in (0, 1):
            got = relr[c, 2 * p].astype(F32) + relr[c, 2 * p + 1].astype(F32)
            rel_s[c, p] = got.astype(BF16)
            at = 2 * c + p
            cp = remote(rel_s.at[c, p], rback.at[c, row_slots + p], s_ry.at[at], r_ry.at[at], far)
            cp.start()
            far_copies.append(cp)
        for p in (0, 1):
            got = fin[c, 2 * p].astype(F32) + fin[c, 2 * p + 1].astype(F32)
            rback[c, row_slots + p] = got.astype(BF16)

    tg_copies = []

    def combine(c):
        for cp in far_copies[2 * c : 2 * c + 2]:
            cp.wait_recv()
        rows = rback[c].reshape(SLOTS * PAIR, CH)
        for kk in (0, 1):
            got = jnp.dot(sel_t[kk], rows, preferred_element_type=F32)
            tgv[c, kk] = got.astype(BF16)
        at = pl.ds(pl.multiple_of(k * HALF + c * CH, CH), CH)
        cp = remote(tgv.at[c, 1 - k], tg_out.at[:, at], s_tg.at[c], r_tg.at[c], sib)
        cp.start()
        tg_copies.append(cp)
        tg_out[:, at] = tgv[c, k]

    for t in range(4):
        for r in range(NR):
            if t < 3 or r < NR // 2:
                a_up[t][r].wait_recv()
                if t < 2 or (t == 2 and r < NR // 2):
                    a_up[t + 1][r].start()
                use(1 + t, below[t + 1], r)
            if t < 3 or r >= NR // 2:
                a_dn[t][r].wait_recv()
                if t < 2 or (t == 2 and r >= NR // 2):
                    a_dn[t + 1][r].start()
                use(5 + t if t < 3 else 4, above[t + 1], r)
        if t == 0:
            relay_back(0)
            relay_back(1)
        if t == 1:
            relay_back(2)
            relay_back(3)
            combine(0)
        if t == 2:
            combine(1)
            combine(2)
    combine(3)

    for cp in tg_copies + d_copies:
        cp.wait()
    for r in toks + grads:
        r.end()
    for cp in far_copies:
        cp.wait_send()
    for sent in r_copies + y_copies:
        for cp in sent:
            cp.wait_send()
    for t in range(4):
        for r in range(NR):
            low = r < NR // 2
            if t > 0 or low:
                downs[t][r].wait_send()
            if t > 0 or not low:
                ups[t][r].wait_send()
            if t < 3 or low:
                a_up[t][r].wait_send()
            if t < 3 or not low:
                a_dn[t][r].wait_send()


def store(*refs):
    sems = refs[-1]
    copies = [pltpu.make_async_copy(refs[i], refs[4 + i], sems.at[i]) for i in range(4)]
    for cp in copies:
        cp.start()
    for cp in copies:
        cp.wait()


def step(tokens, expert_ids, gate_probs, placement, gate_weight, up_weight, down_weight,
         out_grad, moment_first, moment_second):
    def vm(*shape, dtype=BF16):
        return pltpu.VMEM(shape, dtype)

    dma = lambda n: pltpu.SemaphoreType.DMA((n,))
    anywhere = pl.BlockSpec(memory_space=pl.ANY)
    outs = pl.pallas_call(
        body,
        out_shape=(
            vm(TOK, D), vm(1, HU, D), vm(2, HU, SHARE, dtype=F32), vm(2, HU, SHARE, dtype=F32),
        ),
        in_specs=[anywhere] * 3 + [pl.BlockSpec(memory_space=pltpu.SMEM)] + [anywhere] * 6,
        out_specs=(pl.BlockSpec(memory_space=pltpu.VMEM),) * 4,
        scratch_shapes=[
            vm(2, NTC, TOK, TCH), vm(2, NZ, TOK, SHARE),
            vm(2, 8, TOK, dtype=jnp.int32), vm(2, 8, TOK, dtype=F32),
            vm(2, TOK, SLOTS * PAIR),
            vm(NTC, SLOTS, PAIR, TCH), vm(NC, SLOTS, PAIR, CH),
            vm(NTC, 2, PAIR, TCH), vm(NC, 2, PAIR, CH),
            vm(2, NTC, CHIPS, PAIR, TCH), vm(2, NC, CHIPS, PAIR, CH),
            vm(HU, D), vm(HU, D), vm(HU, D),
            vm(2, HU, SHARE, dtype=F32), vm(2, HU, SHARE, dtype=F32),
            vm(HU, ROWS), vm(ROWS, HU, dtype=F32), vm(ROWS, HU), vm(ROWS, HU),
            vm(NC, CHIPS, PAIR, CH), vm(NC, CHIPS, PAIR, CH),
            vm(NC, CHIPS, PAIR, CH, dtype=F32),
            vm(NC, 6, PAIR, CH), vm(NC, NX, PAIR, CH), vm(NC, NX, PAIR, CH),
            vm(NC, 2, PAIR, CH), vm(NC, SLOTS, PAIR, CH), vm(NC, 2, TOK, CH),
            vm(8, 128, dtype=jnp.int32), vm(8, 128, dtype=jnp.int32),
            vm(NZ, NR, PIECE, SHARE), vm(NZ, NR, PIECE, SHARE), vm(NZ, NR, PIECE, SHARE),
            vm(4, NR, 2, PIECE, SHARE), vm(4, NR, 2, PIECE, SHARE),
            vm(4, NR, 2, PIECE, SHARE), vm(4, NR, 2, PIECE, SHARE),
            vm(NZ, NR, 2, PIECE, SHARE), vm(NZ, NR, PIECE, SHARE),
            dma(16 + NTC), dma(11 + NTC), dma(11 + NTC),
            dma(2 * NTC), dma(2 * NTC), dma(2 * NTC), dma(6 * NTC), dma(6 * NTC), dma(8 * NTC),
            dma(8 * NTC),
            dma(2 * NC), dma(2 * NC), dma(2 * NC), dma(6 * NC), dma(6 * NC), dma(8 * NC),
            dma(8 * NC),
            dma(NC), dma(NC), dma(6 * NC), dma(6 * NC), dma(2 * NC), dma(2 * NC), dma(NC), dma(NC),
            dma(1), dma(1), dma(NZ * NR), dma(NZ * NR),
            dma(4 * NR), dma(4 * NR), dma(4 * NR), dma(4 * NR),
            dma(4 * NR), dma(4 * NR), dma(4 * NR), dma(4 * NR), dma(NZ * NR), dma(NZ * NR),
        ],
        compiler_params=pltpu.CompilerParams(
            collective_id=0, has_side_effects=True, vmem_limit_bytes=60 * 2**20
        ),
    )(tokens, expert_ids.T, gate_probs.T, placement, jnp.swapaxes(gate_weight, 1, 2),
      jnp.swapaxes(up_weight, 1, 2), down_weight, out_grad, moment_first, moment_second)
    return pl.pallas_call(
        store,
        out_shape=tuple(jax.ShapeDtypeStruct(o.shape, o.dtype) for o in outs),
        in_specs=[pl.BlockSpec(memory_space=pltpu.VMEM)] * 4,
        out_specs=(anywhere,) * 4,
        scratch_shapes=[dma(4)],
        compiler_params=pltpu.CompilerParams(vmem_limit_bytes=2**20),
    )(*[pltpu.with_memory_space_constraint(o, pltpu.VMEM) for o in outs])


def solution(mesh):
    return jax.shard_map(
        step,
        mesh=mesh,
        in_specs=(
            P(("grp", "ep"), None),
            P(("grp", "ep"), None),
            P(("grp", "ep"), None),
            P("grp", None),
            P("grp", None, "ep"),
            P("grp", None, "ep"),
            P("grp", "ep", None),
            P(("grp", "ep"), None),
            P(None, "ep", "grp"),
            P(None, "ep", "grp"),
        ),
        out_specs=(
            P(("grp", "ep"), None),
            P("grp", "ep", None),
            P(None, "ep", "grp"),
            P(None, "ep", "grp"),
        ),
        check_vma=False,
    )
```
